32 devices in a mesh: gx: 8 (over y, x, core), gy: 4 (over z).
Axes of the slice: x: 2, y: 2, z: 4, core: 2. Of those that a mesh axis runs over, the one named last changes fastest.
Arguments:
- modes: float32 [4, 32, 2048], P(None, 'gx', 'gy'), may hold values from -6 to 6
- directions: float32 [4, 32, 2048], P(None, 'gx', 'gy'), may hold values from -6 to 6
- locked: float32 [60, 32, 2048], P(None, 'gx', 'gy'), may hold values from -9 to 9
- perm_class: int32 [32, 2048], P('gx', 'gy'), may hold values from 0 to 15
- perm_table: float32 [16], replicated, may hold values from 0.01 to 1
- locked_count: int32 [1], replicated, may hold values from 30 to 60
Outputs:
- new_modes: float32 [4, 32, 2048], P(None, 'gx', 'gy')
- new_directions: float32 [4, 32, 2048], P(None, 'gx', 'gy')
- ritz_values: float32 [4], replicated
- locked_correlation: float32 [60, 4], replicated
The draws below stay inside these ranges and needn't reach their ends.
All inputs are finite; a program needn't handle non-finite values.
Results may differ from the reference program's by a relative error of at most 0.0003.
Values sent between devices are 32-bit elements; how exact they have to be, the bound alone decides.
A program may use at most 64 MiB of HBM per device.

```python
import math
import jax
import jax.numpy as jnp
from jax import lax

NZ = 64
ACTIVE = 4
LOCKED = 60
NCLASS = 16
SWEEPS = 3
RITZ = 3
NX = 32
NY = 32


def shared_base(key):
    extent = (ACTIVE, NX, NY * NZ)
    return jnp.clip(jax.random.normal(jax.random.fold_in(key, 11), extent, jnp.float32), -6.0, 6.0)


def draw_modes(key, part):
    return shared_base(key)


def draw_locked(key, part):
    base_field = shared_base(key)
    extent = (LOCKED, NX, NY * NZ)
    noise = jnp.clip(jax.random.normal(jax.random.fold_in(key, 12), extent, jnp.float32), -6.0, 6.0)
    return noise + 0.5 * jnp.tile(base_field, (LOCKED // ACTIVE, 1, 1))


def set_ends(drawn, rng, smallest, largest):
    shape = drawn.shape
    spot = [jax.random.randint(jax.random.fold_in(rng, axis), (), 0, shape[axis]) for axis in range(len(shape))]
    drawn = drawn.at[tuple(spot)].set(smallest)
    longest = shape.index(max(shape))
    spot[longest] = (spot[longest] + 1) % shape[longest]
    return drawn.at[tuple(spot)].set(largest)


def steps_of(key, shape, shards, smallest, high):
    gain, own = 1.0, jax.random.fold_in(key, 6)
    for axis_at, parts in shards:
        heights = jnp.exp(jax.random.uniform(jax.random.fold_in(own, axis_at), (parts,), jnp.float32, smallest / len(shards), high / len(shards)))
        gain = gain * jnp.repeat(heights, shape[axis_at] // parts).reshape([-1 if axis == axis_at else 1 for axis in range(len(shape))])
    return gain


def scatter_about(own_key, shape, spread, reach, cuts=(), kind=jnp.bfloat16):
    result = jax.random.normal(own_key, shape, jnp.float32) * spread
    if len(cuts) > 0:
        result = steps_of(own_key, shape, cuts, -0.22, 0.18) * result
    return jnp.clip(result, min=-reach, max=reach).astype(kind)


def setup_inputs(seed: int = 0) -> dict:
    streams_of = jax.random.split(jax.random.key(seed), 7)
    return {
        "modes": draw_modes(jax.random.fold_in(streams_of[6], 71), 0),
        "directions": scatter_about(streams_of[1], (ACTIVE, NX, NY * NZ), 1.0, 6.0, ((1, 8), (2, 4)), jnp.float32),
        "locked": draw_locked(jax.random.fold_in(streams_of[6], 71), 0),
        "perm_class": set_ends(jax.random.randint(streams_of[3], (NX, NY * NZ), 0, NCLASS), jax.random.fold_in(streams_of[3], 1), 0, NCLASS - 1).astype(jnp.int32),
        "perm_table": jnp.clip(jnp.exp(jax.random.uniform(streams_of[4], (NCLASS,), jnp.float32, math.log(0.01), math.log(1.0))), 0.01, 1.0),
        "locked_count": jax.random.randint(streams_of[5], (1,), LOCKED // 2, LOCKED + 1).astype(jnp.int32),
    }


OMEGA = 0.6
EPSILON = 1e-06
PRECISE = lax.Precision.HIGHEST

def face_value(lower_k, upper_k):
    return jnp.where(lower_k > 0, jnp.where(upper_k > 0, 2.0 * lower_k * upper_k / (lower_k + upper_k), 2.0 * lower_k), 2.0 * upper_k)

def assemble(x_lower, x_upper, y_lower, y_upper, z_lower, z_upper):
    diagonal = x_lower + x_upper + y_lower + y_upper + z_lower + z_upper
    return jnp.stack([diagonal, x_lower, x_upper, y_lower, y_upper, z_lower, z_upper])

def fine_coef(rimmed):
    interior = rimmed[1:-1, 1:-1]
    z_padded = jnp.pad(interior, ((0, 0), (0, 0), (1, 1)))
    x_lower = face_value(rimmed[:-2, 1:-1], interior)
    x_upper = face_value(interior, rimmed[2:, 1:-1])
    y_lower = face_value(rimmed[1:-1, :-2], interior)
    y_upper = face_value(interior, rimmed[1:-1, 2:])
    z_lower = face_value(z_padded[:, :, :-2], interior)
    z_upper = face_value(interior, z_padded[:, :, 2:])
    return assemble(x_lower, x_upper, y_lower, y_upper, z_lower, z_upper)

def pair_sum(blocks, which_dim):
    extent = blocks.shape
    return blocks.reshape(extent[:which_dim] + (extent[which_dim] // 2, 2) + extent[which_dim + 1:]).sum(which_dim + 1)

def coarsen(coeffs):
    x_lower = pair_sum(pair_sum(coeffs[1][0::2], 1), 2)
    x_upper = pair_sum(pair_sum(coeffs[2][1::2], 1), 2)
    y_lower = pair_sum(pair_sum(coeffs[3][:, 0::2], 0), 2)
    y_upper = pair_sum(pair_sum(coeffs[4][:, 1::2], 0), 2)
    z_lower = pair_sum(pair_sum(coeffs[5][:, :, 0::2], 0), 1)
    z_upper = pair_sum(pair_sum(coeffs[6][:, :, 1::2], 0), 1)
    return assemble(x_lower, x_upper, y_lower, y_upper, z_lower, z_upper)

def stencil(rimmed, coeffs):
    center = rimmed[:, 1:-1, 1:-1]
    z_padded = jnp.pad(center, ((0, 0), (0, 0), (0, 0), (1, 1)))
    beside = coeffs[1] * rimmed[:, :-2, 1:-1] + coeffs[2] * rimmed[:, 2:, 1:-1]
    beside = beside + coeffs[3] * rimmed[:, 1:-1, :-2] + coeffs[4] * rimmed[:, 1:-1, 2:]
    beside = beside + coeffs[5] * z_padded[..., :-2] + coeffs[6] * z_padded[..., 2:]
    return coeffs[0] * center - beside

def restrict(field):
    return pair_sum(pair_sum(pair_sum(field, 1), 2), 3)

def prolong(field):
    return jnp.repeat(jnp.repeat(jnp.repeat(field, 2, 1), 2, 2), 2, 3)

def operate(field, coeffs):
    return stencil(jnp.pad(field, ((0, 0), (1, 1), (1, 1), (0, 0))), coeffs)

def line_solve(source, coeffs, shift):
    lower = jnp.transpose(coeffs[3], (0, 2, 1))
    upper = jnp.transpose(coeffs[4], (0, 2, 1))
    others = jnp.transpose(coeffs[1] + coeffs[2] + coeffs[5] + coeffs[6], (0, 2, 1))
    main = lower + upper + shift * others
    below = jnp.concatenate([jnp.zeros_like(lower[..., :1]), -lower[..., 1:]], -1)
    above = jnp.concatenate([-upper[..., :-1], jnp.zeros_like(upper[..., :1])], -1)
    right = jnp.transpose(source, (1, 3, 2, 0))
    solved = lax.linalg.tridiagonal_solve(below, main, above, right)
    return jnp.transpose(solved, (3, 0, 2, 1))

def vcycle(residual, fine_coeffs, middle_coeffs, coarse_coeffs):
    error_fine = OMEGA * residual / fine_coeffs[0]
    source_mid = restrict(residual - operate(error_fine, fine_coeffs))
    error_mid = OMEGA * source_mid / middle_coeffs[0]
    source_low = restrict(source_mid - operate(error_mid, middle_coeffs))
    line_len = source_low.shape[2]
    error_low = line_solve(source_low, coarse_coeffs, 4.0 / float(line_len * line_len))
    for sweep_no in range(SWEEPS - 1):
        error_low = error_low + OMEGA * (source_low - operate(error_low, coarse_coeffs)) / coarse_coeffs[0]
    error_mid = error_mid + prolong(error_low)
    error_mid = error_mid + OMEGA * (source_mid - operate(error_mid, middle_coeffs)) / middle_coeffs[0]
    error_fine = error_fine + prolong(error_mid)
    return error_fine + OMEGA * (residual - operate(error_fine, fine_coeffs)) / fine_coeffs[0]

def rayleigh_ritz(gram_m, gram_a):
    gram_a = 0.5 * (gram_a + gram_a.T)
    chol_m = jnp.linalg.cholesky(gram_m)
    half_solved = lax.linalg.triangular_solve(chol_m, gram_a, left_side=True, lower=True)
    reduced = lax.linalg.triangular_solve(chol_m, half_solved.T, left_side=True, lower=True)
    reduced = 0.5 * (reduced + reduced.T)
    spectral_top = jnp.trace(reduced)
    basis_q = jnp.eye(gram_m.shape[0], ACTIVE, dtype=jnp.float32)
    for ritz_step in range(RITZ):
        raised = spectral_top * basis_q - jnp.dot(reduced, basis_q, precision=PRECISE)
        factor = jnp.linalg.cholesky(jnp.dot(raised.T, raised, precision=PRECISE))
        basis_q = lax.linalg.triangular_solve(factor, raised.T, left_side=True, lower=True).T
    ritz_values = jnp.sum(basis_q * jnp.dot(reduced, basis_q, precision=PRECISE), axis=0)
    coefficients = lax.linalg.triangular_solve(chol_m, basis_q, left_side=True, lower=True, transpose_a=True)
    return (coefficients, ritz_values)

def reference(modes, directions, locked, perm_class, perm_table, locked_count):
    conduct = perm_table[perm_class].reshape(NX, NY, NZ)
    fine_coeffs = fine_coef(jnp.pad(conduct, ((1, 1), (1, 1), (0, 0))))
    middle_coeffs = coarsen(fine_coeffs)
    coarse_coeffs = coarsen(middle_coeffs)
    field_x = modes.reshape(ACTIVE, NX, NY, NZ)
    field_p = directions.reshape(ACTIVE, NX, NY, NZ)
    locked_grid = locked.reshape(LOCKED, NX, NY, NZ)
    cell_count = float(NX * NY * NZ)
    image_x = operate(field_x, fine_coeffs)
    image_p = operate(field_p, fine_coeffs)
    top_sum = jnp.einsum('kxyz,kxyz->k', field_x, image_x, precision=PRECISE)
    norm_sum = jnp.einsum('kxyz,kxyz->k', field_x, field_x, precision=PRECISE)
    rayleigh_q = top_sum / cell_count / (norm_sum / cell_count + EPSILON)
    residual = image_x - rayleigh_q[:, None, None, None] * field_x
    in_use = (jnp.arange(LOCKED, dtype=jnp.int32) < locked_count[0])[:, None]
    coupling = jnp.where(in_use, jnp.einsum('jxyz,kxyz->jk', locked_grid, residual, precision=PRECISE) / cell_count, 0.0)
    residual = residual - jnp.einsum('jk,jxyz->kxyz', coupling, locked_grid, precision=PRECISE)
    precond = vcycle(residual, fine_coeffs, middle_coeffs, coarse_coeffs)
    correlation = jnp.where(in_use, jnp.einsum('jxyz,kxyz->jk', locked_grid, precond, precision=PRECISE) / cell_count, 0.0)
    projected = precond - jnp.einsum('jk,jxyz->kxyz', correlation, locked_grid, precision=PRECISE)
    image_w = operate(projected, fine_coeffs)
    trial = jnp.concatenate([field_x, projected, field_p], 0)
    images = jnp.concatenate([image_x, image_w, image_p], 0)
    gram_m = jnp.einsum('axyz,bxyz->ab', trial, trial, precision=PRECISE) / cell_count
    gram_a = jnp.einsum('axyz,bxyz->ab', trial, images, precision=PRECISE) / cell_count
    coefficients, ritz_values = rayleigh_ritz(gram_m, gram_a)
    new_modes = jnp.einsum('ak,axyz->kxyz', coefficients, trial, precision=PRECISE)
    new_directions = jnp.einsum('ak,axyz->kxyz', coefficients[ACTIVE:], trial[ACTIVE:], precision=PRECISE)
    return (new_modes.reshape(ACTIVE, NX, NY * NZ), new_directions.reshape(ACTIVE, NX, NY * NZ), ritz_values, correlation)
```

```python
import functools

import jax
import jax.numpy as jnp
from jax import lax
from jax.experimental import pallas as pl
from jax.experimental.pallas import tpu as pltpu
from jax.sharding import PartitionSpec as P

NZ = 64
ACTIVE = 4
SWEEPS = 3
RITZ = 3
OMEGA = 0.6
EPSILON = 1e-06
PRECISE = lax.Precision.HIGHEST
F32 = jnp.float32
REACH = SWEEPS


def iota(shape, dim):
    return lax.broadcasted_iota(jnp.int32, shape, dim)


def nt(a, b):
    return lax.dot_general(a, b, (((1,), (1,)), ((), ())), precision=PRECISE, preferred_element_type=F32)


def nn(a, b):
    return lax.dot_general(a, b, (((1,), (0,)), ((), ())), precision=PRECISE, preferred_element_type=F32)


def lanes(u, by):
    return pltpu.roll(u, by % 128, u.ndim - 1)


def subs(u, by):
    return pltpu.roll(u, by % 8, u.ndim - 2)


def face_value(a, b):
    both = (a > 0) & (b > 0)
    return jnp.where(both, 2.0 * a * b / jnp.where(both, a + b, 1.0), 2.0 * (a + b))


class Marks:
    def __init__(self):
        lane = iota((8, 128), 1)
        sub = iota((8, 128), 0)
        self.lane = lane
        self.sub = sub
        self.z = lane % NZ
        self.half0 = lane < 64
        self.par0 = sub < 4
        self.even = lane % 2 == 0
        self.quad = lane % 4 < 2


def neighbours(m, u):
    inner = u[1:-1, 1:-1]
    zl = jnp.where(m.z == 0, 0.0, lanes(inner, 1))
    zu = jnp.where(m.z == NZ - 1, 0.0, lanes(inner, -1))
    flip = lanes(u[1:-1], 64)
    yl = jnp.where(m.half0, flip[:, :-2], flip[:, 1:-1])
    yu = jnp.where(m.half0, flip[:, 1:-1], flip[:, 2:])
    turn = subs(u[:, 1:-1], 4)
    xl = jnp.where(m.par0, turn[:-2], turn[1:-1])
    xu = jnp.where(m.par0, turn[1:-1], turn[2:])
    return xl, xu, yl, yu, zl, zu


def total(parts):
    out = parts[0]
    for part in parts[1:]:
        out = out + part
    return out


def fine_coef(m, k):
    inner = k[1:-1, 1:-1]
    faces = [face_value(near, inner) for near in neighbours(m, k)]
    return [total(faces)] + faces


def stencil(m, u, coef):
    near = neighbours(m, u)
    return coef[0] * u[1:-1, 1:-1] - total([c * v for c, v in zip(coef[1:], near)])


def inverse(diag, inside):
    return jnp.where(inside, OMEGA / jnp.where(inside, diag, 1.0), 0.0)


def pair_x(u):
    return u + subs(u, 4)


def pair_y(u):
    return u + lanes(u, 64)


def pair_z(m, u):
    return u + jnp.where(m.even, lanes(u, -1), lanes(u, 1))


def pair_z2(m, u):
    return u + jnp.where(m.quad, lanes(u, -2), lanes(u, 2))


def middle_coef(m, c):
    xl = pair_z(m, pair_y(jnp.where(m.par0, c[1], subs(c[1], 4))))
    xu = pair_z(m, pair_y(jnp.where(m.par0, subs(c[2], 4), c[2])))
    yl = pair_z(m, pair_x(jnp.where(m.half0, c[3], lanes(c[3], 64))))
    yu = pair_z(m, pair_x(jnp.where(m.half0, lanes(c[4], 64), c[4])))
    zl = pair_y(pair_x(jnp.where(m.even, c[5], lanes(c[5], 1))))
    zu = pair_y(pair_x(jnp.where(m.even, lanes(c[6], -1), c[6])))
    faces = [xl, xu, yl, yu, zl, zu]
    return [total(faces)] + faces


def middle_stencil(m, u, coef):
    inner = u[1:-1, 1:-1]
    zl = jnp.where(m.z < 2, 0.0, lanes(inner, 2))
    zu = jnp.where(m.z >= NZ - 2, 0.0, lanes(inner, -2))
    near = [u[:-2, 1:-1], u[2:, 1:-1], u[1:-1, :-2], u[1:-1, 2:], zl, zu]
    return coef[0] * inner - total([c * v for c, v in zip(coef[1:], near)])


def coarse_pack(m, mid):
    _, xl, xu, yl, yu, zl, zu = mid
    out = jnp.zeros((8, 128), F32)
    for q in range(2):
        a, b = 2 * q, 2 * q + 1
        faces = [
            pair_z2(m, xl[0, a] + xl[0, b]),
            pair_z2(m, xu[1, a] + xu[1, b]),
            pair_z2(m, yl[0, a] + yl[1, a]),
            pair_z2(m, yu[0, b] + yu[1, b]),
        ]
        low = zl[0, a] + zl[0, b] + zl[1, a] + zl[1, b]
        high = zu[0, a] + zu[0, b] + zu[1, a] + zu[1, b]
        faces.append(jnp.where(m.quad, low, lanes(low, 2)))
        faces.append(jnp.where(m.quad, lanes(high, -2), high))
        for k in range(6):
            spot = (m.sub == 4 * q + k % 4) & (m.half0 if k < 4 else ~m.half0)
            out = jnp.where(spot, faces[k], out)
    return out


def flat(u):
    return jnp.concatenate([u[x, y] for x in range(2) for y in range(4)], axis=1)


def unflat(u):
    tiles = [u[:, 128 * i : 128 * (i + 1)] for i in range(8)]
    return jnp.stack([jnp.stack(tiles[:4]), jnp.stack(tiles[4:])])


def fold_locked(m, g):
    g = jnp.where(m.par0 == m.half0, g, 0.0)
    return pair_y(pair_x(g))


def spread_locked(m, c):
    return jnp.where(m.par0 == m.half0, c, 0.0)


def kernel(
    ngx,
    ngy,
    modes_ref,
    dirs_ref,
    locked_ref,
    class_ref,
    table_ref,
    count_ref,
    new_modes_ref,
    new_dirs_ref,
    ritz_ref,
    corr_ref,
    kh,
    xp,
    e0h,
    e1h,
    wh,
    ccg,
    r2g,
    e2s,
    lst,
    by1,
    bx1,
    by2,
    bx2,
    by3,
    bx3,
    hs,
    hr,
    rs,
    rr,
    cs,
    cr,
):
    m = Marks()
    gx, gy = lax.axis_index("gx"), lax.axis_index("gy")
    count = ngx * ngy
    cells = float(4 * 512 * count)
    pending = []

    for buf in (kh, xp, e0h, e1h, wh, ccg, r2g, e2s):
        buf[...] = jnp.zeros(buf.shape, F32)

    barrier = pltpu.get_barrier_semaphore()
    me = gx * ngy + gy

    def greet(i, carry):
        other = lax.rem(me + i, count)
        pl.semaphore_signal(
            barrier, inc=1, device_id=(other // ngy, lax.rem(other, ngy)), device_id_type=pl.DeviceIdType.MESH
        )
        return carry

    lax.fori_loop(1, count, greet, 0)

    def remote(src, dst, send, recv, tx, ty):
        return pltpu.make_async_remote_copy(
            src_ref=src, dst_ref=dst, send_sem=send, recv_sem=recv, device_id=(tx, ty),
            device_id_type=pl.DeviceIdType.MESH,
        )

    def inside(tx, ty):
        return (tx >= 0) & (tx < ngx) & (ty >= 0) & (ty < ngy)

    def halo(slot, view, w, corners):
        def span(d, n):
            if d > 0:
                return pl.ds(n, w), pl.ds(0, w)
            if d < 0:
                return pl.ds(w, w), pl.ds(w + n, w)
            return pl.ds(w, n), pl.ds(w, n)

        copies = []
        for dx in (-1, 0, 1):
            for dy in (-1, 0, 1):
                if (dx, dy) == (0, 0) or (dx and dy and not corners):
                    continue
                (sx, tx), (sy, ty) = span(dx, 2), span(dy, 4)
                n = (dx + 1) * 3 + dy + 1
                copy = remote(view(sx, sy), view(tx, ty), hs.at[slot, n], hr.at[slot, n], gx + dx, gy + dy)
                to, frm = inside(gx + dx, gy + dy), inside(gx - dx, gy - dy)
                pl.when(to)(copy.start)
                copies.append((copy, frm))
                pending.append((copy, to))

        def arrive():
            for copy, frm in copies:
                pl.when(frm)(copy.wait_recv)

        return arrive

    def share(slot, buf, mine, n, axis, view):
        copies = []
        for i in range(1, n):
            to, frm = lax.rem(mine + i, n), lax.rem(mine + n - i, n)
            where = (gx, to) if axis == "gy" else (to, gy)
            back = (gx, frm) if axis == "gy" else (frm, gy)
            copy = remote(view(buf, mine), view(buf, mine), rs.at[slot, i], rr.at[slot, i], *where)
            copy.start()
            pending.append((copy, None))
            copies.append(remote(view(buf, frm), view(buf, frm), rs.at[slot, i], rr.at[slot, i], *back))

        def arrive():
            for copy in copies:
                copy.wait_recv()

        return arrive

    def reduce_start(slot, val, bufy):
        bufy[gy] = val
        return share(slot, bufy, gy, ngy, "gy", lambda b, i: b.at[i])

    def reduce_end(slot, first, bufy, bufx):
        first()
        bufx[gx] = total([bufy[j] for j in range(ngy)])
        share(slot + 1, bufx, gx, ngx, "gx", lambda b, i: b.at[i])()
        return total([bufx[j] for j in range(ngx)])

    def gather_start(slot, buf, val):
        buf[REACH, gy] = val
        return share(slot, buf, gy, ngy, "gy", lambda b, i: b.at[REACH, i])

    def gather_next(slot, first, buf):
        first()
        copies = []
        for d in range(-REACH, REACH + 1):
            if d == 0:
                continue
            copy = remote(
                buf.at[REACH], buf.at[REACH - d], cs.at[slot, d + REACH], cr.at[slot, d + REACH], gx + d, gy
            )
            to, frm = inside(gx + d, gy), inside(gx - d, gy)
            pl.when(to)(copy.start)
            copies.append((copy, frm))
            pending.append((copy, to))

        def arrive():
            for copy, frm in copies:
                pl.when(frm)(copy.wait_recv)

        return arrive

    classes = class_ref[...]
    conduct = jnp.zeros(classes.shape, F32)
    for c in range(table_ref.shape[0]):
        conduct = jnp.where(classes == c, table_ref[c], conduct)
    for x in range(4):
        for y in range(4):
            cut = slice(128 * y, 128 * (y + 1))
            rows = pl.ds(4 * (x % 2), 4)
            kh[2 + x // 2, 2 + y, rows, :] = jnp.broadcast_to(conduct[x : x + 1, cut], (4, 128))
            xp[0, 1 + x // 2, 1 + y, rows, :] = modes_ref[:, x, cut]
            xp[1, 1 + x // 2, 1 + y, rows, :] = dirs_ref[:, x, cut]
    pl.semaphore_wait(barrier, count - 1)
    arrive_k = halo(0, lambda a, b: kh.at[a, b], 2, True)
    arrive_xp = halo(1, lambda a, b: xp.at[:, a, b], 1, False)

    nl = locked_ref.shape[0]
    for x in range(4):
        for y in range(4):
            cut = slice(128 * y, 128 * (y + 1))
            to = pl.ds(128 * ((x // 2) * 4 + y), 128)
            lst[pl.ds(64 * (x % 2), nl), to] = locked_ref[:, x, cut]
            lst[pl.ds(64 * (x % 2) + nl, 4), to] = modes_ref[:, x, cut]

    own_x = xp[0, 1:3, 1:5]
    own_p = xp[1, 1:3, 1:5]
    x8 = flat(own_x)
    mode_dots = fold_locked(m, nt(x8, lst[...]))

    arrive_k()
    arrive_xp()
    own_coef = fine_coef(m, kh[1:5, 1:7])
    image_x = stencil(m, xp[0], own_coef)
    image_x8 = flat(image_x)
    image_dots = fold_locked(m, nt(image_x8, lst[...]))
    first = reduce_start(0, jnp.where(m.half0, image_dots, mode_dots), by1)

    wide = fine_coef(m, kh[...])
    in_grid = kh[1:5, 1:7] > 0
    dinv0 = inverse(wide[0], in_grid)
    mid = middle_coef(m, wide)
    dinv1 = inverse(mid[0], in_grid)
    own_mid = [c[1:3, 1:5] for c in mid]
    first_c = gather_start(6, ccg, coarse_pack(m, own_mid))
    image_p = stencil(m, xp[1], own_coef)

    sums = reduce_end(0, first, by1, bx1)
    arrive_c = gather_next(0, first_c, ccg)

    f_of = m.sub % 4
    top = jnp.sum(jnp.where(m.lane == nl + f_of, sums, 0.0), axis=1, keepdims=True)
    norm = jnp.sum(jnp.where(m.lane == 64 + nl + f_of, sums, 0.0), axis=1, keepdims=True)
    rayleigh = top / cells / (norm / cells + EPSILON)
    swapped = lanes(sums, 64)
    image_sum = jnp.where(m.half0, sums, swapped)
    mode_sum = jnp.where(m.half0, swapped, sums)
    j_of = m.lane % 64
    in_use = (j_of < count_ref[0]) & (j_of < nl)
    coupling = jnp.where(in_use, (image_sum - mode_sum * rayleigh) / cells, 0.0)
    coupling = jnp.where(j_of == nl + f_of, rayleigh, coupling)
    residual = image_x - unflat(nn(spread_locked(m, coupling), lst[...]))

    e0h[1:3, 1:5] = residual * dinv0[1:3, 1:5]
    arrive_e0 = halo(2, lambda a, b: e0h.at[a, b], 1, False)
    arrive_c()
    lines = 2 * ngy
    shift = 4.0 / float(lines * lines)
    faces = []
    for y in range(lines):
        tile = ccg[:, y // 2]
        other = lanes(tile, 64)
        low, high = jnp.where(m.half0, tile, other), jnp.where(m.half0, other, tile)
        row = 4 * (y % 2)
        one = []
        for k in range(6):
            src = low if k < 4 else high
            one.append(jnp.broadcast_to(src[:, row + k % 4 : row + k % 4 + 1], (2 * REACH + 1, 4, 128)))
        faces.append(one)
    z4 = m.z[:4]
    pivots, uppers, diags, dinv2 = [], [], [], []
    for y in range(lines):
        xl, xu, yl, yu, zl, zu = faces[y]
        diag = xl + xu + yl + yu + zl + zu
        known = diag > 0
        main = yl + yu + shift * (xl + xu + zl + zu)
        if y:
            main = main - yl * uppers[y - 1]
        piv = 1.0 / jnp.where(known, main, 1.0)
        pivots.append(piv)
        uppers.append(yu * piv)
        diags.append(diag)
        dinv2.append(inverse(diag, known))
        faces[y][4] = jnp.where(z4 < 4, 0.0, zl)
        faces[y][5] = jnp.where(z4 >= NZ - 4, 0.0, zu)

    arrive_e0()
    r1 = residual - stencil(m, e0h[...], own_coef)
    r1 = pair_z(m, pair_y(pair_x(r1)))
    e1h[2:4, 2:6] = r1 * dinv1[1:3, 1:5]
    halo(3, lambda a, b: e1h.at[a, b], 2, True)()
    e1_wide = e1h[...]
    r2 = r1 - middle_stencil(m, e1_wide[1:5, 1:7], own_mid)
    r2 = r2[0] + r2[1]
    r2 = jnp.where(m.par0, r2[0] + r2[1], r2[2] + r2[3])
    first_r = gather_start(7, r2g, pair_z2(m, r2))
    gather_next(1, first_r, r2g)()

    source = [r2g[:, y // 2, 4 * (y % 2) : 4 * (y % 2) + 4] for y in range(lines)]
    held = []
    for y in range(lines):
        right = source[y] if y == 0 else source[y] + faces[y][2] * held[y - 1]
        held.append(right * pivots[y])
    for y in range(lines - 2, -1, -1):
        held[y] = held[y] + uppers[y] * held[y + 1]
    for sweep in range(1, SWEEPS):
        nxt = []
        for y in range(lines):
            cut = slice(sweep, 2 * REACH + 1 - sweep)
            c = [f[cut] for f in faces[y]]
            u = held[y]
            mid_u = u[1:-1]
            beside = c[0] * u[:-2] + c[1] * u[2:]
            if y:
                beside = beside + c[2] * held[y - 1][1:-1]
            if y < lines - 1:
                beside = beside + c[3] * held[y + 1][1:-1]
            beside = beside + c[4] * lanes(mid_u, 4) + c[5] * lanes(mid_u, -4)
            off = source[y][cut] - (diags[y][cut] * mid_u - beside)
            nxt.append(mid_u + dinv2[y][cut] * off)
        held = nxt
    for y in range(lines):
        e2s[1 + y] = held[y]
    near = e2s[pl.ds(2 * gy, 4)]
    near = jnp.concatenate([near, near], axis=2)

    e1_wide = jnp.stack(
        [jnp.stack([e1_wide[a, b] + near[b // 2, a // 2] for b in range(8)]) for a in range(6)]
    )
    e1 = e1_wide[1:5, 1:7] + e1h[1:5, 1:7] - dinv1 * middle_stencil(m, e1_wide, mid)
    e0 = e0h[...] + e1
    precond = e0[1:3, 1:5] + e0h[1:3, 1:5] - dinv0[1:3, 1:5] * stencil(m, e0, own_coef)

    precond8 = flat(precond)
    dots = fold_locked(m, nt(precond8, lst[...]))
    sums = reduce_end(2, reduce_start(2, dots, by2), by2, bx2)
    corr = jnp.where(in_use, sums / cells, 0.0)
    corr_ref[...] = corr.T[: corr_ref.shape[0], :ACTIVE]
    projected8 = precond8 - nn(spread_locked(m, corr), lst[...])
    wh[1:3, 1:5] = unflat(projected8)
    halo(4, lambda a, b: wh.at[a, b], 1, False)()
    image_w = stencil(m, wh[...], own_coef)

    trial = jnp.concatenate([x8, projected8, flat(own_p)], axis=0)
    images = jnp.concatenate([image_x8, flat(image_w), flat(image_p)], axis=0)
    mass = nt(trial, trial)
    stiff = 0.5 * (nt(trial, images) + nt(images, trial))
    both = jnp.concatenate([mass, jnp.zeros((24, 8), F32), stiff, jnp.zeros((24, 72), F32)], axis=1)
    row, col = iota((24, 128), 0), iota((24, 128), 1)
    both = jnp.where((row // 4) % 2 == (col // 4) % 2, both, 0.0)
    both = both + jnp.concatenate([subs(both[8 * i : 8 * i + 8], 4) for i in range(3)], axis=0)
    both = both + lanes(both, -4)
    sums = reduce_end(4, reduce_start(4, both, by3), by3, bx3) / cells

    real = row % 8 < 4
    table = jnp.where(real & (col < 64) & (col % 8 < 4), sums, 0.0)
    table = jnp.where(real & (col == row + 64), 1.0, table)
    pivots_at = [8 * g + f for g in range(3) for f in range(4)]

    def eliminate(work, order, rows):
        for k in order:
            pivot = work[k : k + 1, k : k + 1]
            scale = lax.rsqrt(pivot)
            line = work[k : k + 1, :] * scale
            factor = jnp.where(rows > k, work[:, k : k + 1] * scale, 0.0)
            work = jnp.where(rows == k, line, work - factor * line)
        return work

    work = eliminate(table, pivots_at, row)
    half = jnp.where(col < 24, lanes(work, -32), 0.0)
    linv = jnp.where(col < 24, lanes(work, -64), 0.0)
    reduced = 0.5 * (nt(half, linv) + nt(linv, half))
    reduced = jnp.concatenate([reduced, jnp.zeros((24, 104), F32)], axis=1)
    spectral = jnp.sum(jnp.where(row == col, reduced, 0.0), keepdims=True)
    raised = jnp.where((row == col) & real, spectral, 0.0) - reduced
    full = jnp.concatenate([raised, jnp.zeros((104, 128), F32)], axis=0)
    reduced_full = jnp.concatenate([reduced, jnp.zeros((104, 128), F32)], axis=0)
    basis = jnp.where(m.par0, raised[:8], 0.0)
    for step in range(RITZ - 1):
        basis = nn(basis, full)
    square = nt(basis, basis)
    small = jnp.concatenate([square, jnp.zeros((8, 120), F32)], axis=1) + lanes(basis, 32)
    small = eliminate(small, range(4), m.sub)
    basis = jnp.where((m.lane < 24) & m.par0, lanes(small, -32), 0.0)
    ritz = jnp.sum(basis * nn(basis, reduced_full), axis=1, keepdims=True)
    for k in range(ACTIVE):
        ritz_ref[k] = ritz[k, 0]
    linv_full = jnp.concatenate([linv, jnp.zeros((104, 128), F32)], axis=0)
    coef = nn(basis, linv_full)
    coef = coef + lanes(coef, 4)
    coef = coef + subs(coef, 4)
    coef = jnp.where(m.par0 == ((m.lane // 4) % 2 == 0), coef, 0.0)[:, :24]
    modes8 = nn(coef, trial)
    dirs8 = nn(coef[:, 8:], trial[8:])
    for x in range(4):
        for y in range(4):
            cut = slice(128 * y, 128 * (y + 1))
            frm = slice(128 * ((x // 2) * 4 + y), 128 * ((x // 2) * 4 + y + 1))
            rows = slice(4 * (x % 2), 4 * (x % 2) + 4)
            new_modes_ref[:, x, cut] = modes8[rows, frm]
            new_dirs_ref[:, x, cut] = dirs8[rows, frm]

    for copy, to in pending:
        if to is None:
            copy.wait_send()
        else:
            pl.when(to)(copy.wait_send)


def on_device(ngx, ngy, modes, directions, locked, perm_class, perm_table, locked_count):
    vmem = pl.BlockSpec(memory_space=pltpu.VMEM)
    smem = pl.BlockSpec(memory_space=pltpu.SMEM)
    dma = pltpu.SemaphoreType.DMA
    wide = 2 * REACH + 1
    return pl.pallas_call(
        functools.partial(kernel, ngx, ngy),
        out_shape=(
            jax.ShapeDtypeStruct(modes.shape, F32),
            jax.ShapeDtypeStruct(modes.shape, F32),
            jax.ShapeDtypeStruct((ACTIVE,), F32),
            jax.ShapeDtypeStruct((locked.shape[0], ACTIVE), F32),
        ),
        in_specs=[vmem, vmem, vmem, vmem, smem, smem],
        out_specs=(vmem, vmem, smem, vmem),
        scratch_shapes=[
            pltpu.VMEM((6, 8, 8, 128), F32),
            pltpu.VMEM((2, 4, 6, 8, 128), F32),
            pltpu.VMEM((4, 6, 8, 128), F32),
            pltpu.VMEM((6, 8, 8, 128), F32),
            pltpu.VMEM((4, 6, 8, 128), F32),
            pltpu.VMEM((wide, ngy, 8, 128), F32),
            pltpu.VMEM((wide, ngy, 8, 128), F32),
            pltpu.VMEM((2 * ngy + 2, 3, 4, 128), F32),
            pltpu.VMEM((128, 1024), F32),
            pltpu.VMEM((ngy, 8, 128), F32),
            pltpu.VMEM((ngx, 8, 128), F32),
            pltpu.VMEM((ngy, 8, 128), F32),
            pltpu.VMEM((ngx, 8, 128), F32),
            pltpu.VMEM((ngy, 24, 128), F32),
            pltpu.VMEM((ngx, 24, 128), F32),
            dma((5, 9)),
            dma((5, 9)),
            dma((8, max(ngx, ngy))),
            dma((8, max(ngx, ngy))),
            dma((2, wide)),
            dma((2, wide)),
        ],
        compiler_params=pltpu.CompilerParams(
            collective_id=0, has_side_effects=True, vmem_limit_bytes=48 * 1024 * 1024
        ),
    )(modes, directions, locked, perm_class, perm_table, locked_count)


def solution(mesh):
    placed = (
        P(None, "gx", "gy"),
        P(None, "gx", "gy"),
        P(None, "gx", "gy"),
        P("gx", "gy"),
        P(),
        P(),
    )
    return jax.shard_map(
        functools.partial(on_device, mesh.shape["gx"], mesh.shape["gy"]),
        mesh=mesh,
        in_specs=placed,
        out_specs=(P(None, "gx", "gy"), P(None, "gx", "gy"), P(), P()),
        check_vma=False,
    )
```

```python
import functools

import jax
import jax.numpy as jnp
from jax import lax
from jax.experimental import pallas as pl
from jax.experimental.pallas import tpu as pltpu
from jax.sharding import PartitionSpec as P

NZ = 64
ACTIVE = 4
SWEEPS = 3
RITZ = 3
OMEGA = 0.6
EPSILON = 1e-06
PRECISE = lax.Precision.HIGHEST
F32 = jnp.float32
REACH = SWEEPS


def iota(shape, dim):
    return lax.broadcasted_iota(jnp.int32, shape, dim)


def nt(a, b):
    return lax.dot_general(a, b, (((1,), (1,)), ((), ())), precision=PRECISE, preferred_element_type=F32)


def nn(a, b):
    return lax.dot_general(a, b, (((1,), (0,)), ((), ())), precision=PRECISE, preferred_element_type=F32)


def lanes(u, by):
    return pltpu.roll(u, by % 128, u.ndim - 1)


def subs(u, by):
    return pltpu.roll(u, by % 8, u.ndim - 2)


def face_value(a, b):
    both = (a > 0) & (b > 0)
    return jnp.where(both, 2.0 * a * b / jnp.where(both, a + b, 1.0), 2.0 * (a + b))


BF16 = jnp.bfloat16


def split(a):
    high = a.astype(BF16)
    return high, (a - high.astype(F32)).astype(BF16)


def dot_split(a, b_high, b_low, dims):
    rows = a.shape[0]
    high = a.astype(BF16).astype(F32)
    stack = jnp.concatenate([high, a - high], axis=0).astype(BF16)
    dims = (dims, ((), ()))
    one = lax.dot_general(stack, b_high, dims, preferred_element_type=F32)
    two = lax.dot_general(high.astype(BF16), b_low, dims, preferred_element_type=F32)
    return one[:rows] + (one[rows:] + two)


NT = ((1,), (1,))
NN = ((1,), (0,))


class Marks:
    def __init__(self):
        lane = iota((8, 128), 1)
        sub = iota((8, 128), 0)
        self.lane = lane
        self.sub = sub
        self.z = lane % NZ
        self.half0 = lane < 64
        self.par0 = sub < 4
        self.even = lane % 2 == 0
        self.quad = lane % 4 < 2


def neighbours(m, u):
    inner = u[1:-1, 1:-1]
    zl = jnp.where(m.z == 0, 0.0, lanes(inner, 1))
    zu = jnp.where(m.z == NZ - 1, 0.0, lanes(inner, -1))
    flip = lanes(u[1:-1], 64)
    yl = jnp.where(m.half0, flip[:, :-2], flip[:, 1:-1])
    yu = jnp.where(m.half0, flip[:, 1:-1], flip[:, 2:])
    turn = subs(u[:, 1:-1], 4)
    xl = jnp.where(m.par0, turn[:-2], turn[1:-1])
    xu = jnp.where(m.par0, turn[1:-1], turn[2:])
    return xl, xu, yl, yu, zl, zu


def total(parts):
    out = parts[0]
    for part in parts[1:]:
        out = out + part
    return out


def fine_coef(m, k):
    inner = k[1:-1, 1:-1]
    faces = [face_value(near, inner) for near in neighbours(m, k)]
    return [total(faces)] + faces


def stencil(m, u, coef):
    near = neighbours(m, u)
    return coef[0] * u[1:-1, 1:-1] - total([c * v for c, v in zip(coef[1:], near)])


def inverse(diag, inside):
    return jnp.where(inside, OMEGA / jnp.where(inside, diag, 1.0), 0.0)


def pair_x(u):
    return u + subs(u, 4)


def pair_y(u):
    return u + lanes(u, 64)


def pair_z(m, u):
    return u + jnp.where(m.even, lanes(u, -1), lanes(u, 1))


def pair_z2(m, u):
    return u + jnp.where(m.quad, lanes(u, -2), lanes(u, 2))


def middle_coef(m, c):
    xl = pair_z(m, pair_y(jnp.where(m.par0, c[1], subs(c[1], 4))))
    xu = pair_z(m, pair_y(jnp.where(m.par0, subs(c[2], 4), c[2])))
    yl = pair_z(m, pair_x(jnp.where(m.half0, c[3], lanes(c[3], 64))))
    yu = pair_z(m, pair_x(jnp.where(m.half0, lanes(c[4], 64), c[4])))
    zl = pair_y(pair_x(jnp.where(m.even, c[5], lanes(c[5], 1))))
    zu = pair_y(pair_x(jnp.where(m.even, lanes(c[6], -1), c[6])))
    faces = [xl, xu, yl, yu, zl, zu]
    return [total(faces)] + faces


def middle_stencil(m, u, coef):
    inner = u[1:-1, 1:-1]
    zl = jnp.where(m.z < 2, 0.0, lanes(inner, 2))
    zu = jnp.where(m.z >= NZ - 2, 0.0, lanes(inner, -2))
    near = [u[:-2, 1:-1], u[2:, 1:-1], u[1:-1, :-2], u[1:-1, 2:], zl, zu]
    return coef[0] * inner - total([c * v for c, v in zip(coef[1:], near)])


def coarse_pack(m, mid):
    _, xl, xu, yl, yu, zl, zu = mid
    out = jnp.zeros((8, 128), F32)
    for q in range(2):
        a, b = 2 * q, 2 * q + 1
        faces = [
            pair_z2(m, xl[0, a] + xl[0, b]),
            pair_z2(m, xu[1, a] + xu[1, b]),
            pair_z2(m, yl[0, a] + yl[1, a]),
            pair_z2(m, yu[0, b] + yu[1, b]),
        ]
        low = zl[0, a] + zl[0, b] + zl[1, a] + zl[1, b]
        high = zu[0, a] + zu[0, b] + zu[1, a] + zu[1, b]
        faces.append(jnp.where(m.quad, low, lanes(low, 2)))
        faces.append(jnp.where(m.quad, lanes(high, -2), high))
        for k in range(6):
            spot = (m.sub == 4 * q + k % 4) & (m.half0 if k < 4 else ~m.half0)
            out = jnp.where(spot, faces[k], out)
    return out


def flat(u):
    return jnp.concatenate([u[x, y] for x in range(2) for y in range(4)], axis=1)


def unflat(u):
    tiles = [u[:, 128 * i : 128 * (i + 1)] for i in range(8)]
    return jnp.stack([jnp.stack(tiles[:4]), jnp.stack(tiles[4:])])


def fold_locked(m, g):
    g = jnp.where(m.par0 == m.half0, g, 0.0)
    return pair_y(pair_x(g))


def spread_locked(m, c):
    return jnp.where(m.par0 == m.half0, c, 0.0)


def kernel(
    ngx,
    ngy,
    modes_hbm,
    dirs_hbm,
    locked_hbm,
    class_hbm,
    table_ref,
    count_ref,
    new_modes_ref,
    new_dirs_ref,
    ritz_ref,
    corr_ref,
    kh,
    xp,
    e0h,
    e1h,
    wh,
    ccg,
    r2g,
    e2s,
    lst,
    l_high,
    l_low,
    modes_ref,
    dirs_ref,
    locked_ref,
    class_ref,
    ins,
    by1,
    bx1,
    by2,
    bx2,
    by3,
    bx3,
    hs,
    hr,
    rs,
    rr,
    cs,
    cr,
):
    loads = [
        pltpu.make_async_copy(src, dst, ins.at[i])
        for i, (src, dst) in enumerate(
            [(class_hbm, class_ref), (modes_hbm, modes_ref), (dirs_hbm, dirs_ref), (locked_hbm, locked_ref)]
        )
    ]
    for load in loads:
        load.start()
    m = Marks()
    gx, gy = lax.axis_index("gx"), lax.axis_index("gy")
    count = ngx * ngy
    cells = float(4 * 512 * count)
    pending = []

    for buf in (kh, xp, e0h, e1h, wh, ccg, r2g, e2s):
        buf[...] = jnp.zeros(buf.shape, F32)

    barrier = pltpu.get_barrier_semaphore()
    me = gx * ngy + gy

    def greet(i, carry):
        other = lax.rem(me + i, count)
        pl.semaphore_signal(
            barrier, inc=1, device_id=(other // ngy, lax.rem(other, ngy)), device_id_type=pl.DeviceIdType.MESH
        )
        return carry

    lax.fori_loop(1, count, greet, 0)

    def remote(src, dst, send, recv, tx, ty):
        return pltpu.make_async_remote_copy(
            src_ref=src, dst_ref=dst, send_sem=send, recv_sem=recv, device_id=(tx, ty),
            device_id_type=pl.DeviceIdType.MESH,
        )

    def inside(tx, ty):
        return (tx >= 0) & (tx < ngx) & (ty >= 0) & (ty < ngy)

    def halo(slot, view, w, corners):
        def span(d, n):
            if d > 0:
                return pl.ds(n, w), pl.ds(0, w)
            if d < 0:
                return pl.ds(w, w), pl.ds(w + n, w)
            return pl.ds(w, n), pl.ds(w, n)

        copies = []
        for dx in (-1, 0, 1):
            for dy in (-1, 0, 1):
                if (dx, dy) == (0, 0) or (dx and dy and not corners):
                    continue
                (sx, tx), (sy, ty) = span(dx, 2), span(dy, 4)
                n = (dx + 1) * 3 + dy + 1
                copy = remote(view(sx, sy), view(tx, ty), hs.at[slot, n], hr.at[slot, n], gx + dx, gy + dy)
                to, frm = inside(gx + dx, gy + dy), inside(gx - dx, gy - dy)
                pl.when(to)(copy.start)
                copies.append((copy, frm))
                pending.append((copy, to))

        def arrive():
            for copy, frm in copies:
                pl.when(frm)(copy.wait_recv)

        return arrive

    def share(slot, buf, mine, n, axis, view):
        copies = []
        for i in range(1, n):
            to, frm = lax.rem(mine + i, n), lax.rem(mine + n - i, n)
            where = (gx, to) if axis == "gy" else (to, gy)
            back = (gx, frm) if axis == "gy" else (frm, gy)
            copy = remote(view(buf, mine), view(buf, mine), rs.at[slot, i], rr.at[slot, i], *where)
            copy.start()
            pending.append((copy, None))
            copies.append(remote(view(buf, frm), view(buf, frm), rs.at[slot, i], rr.at[slot, i], *back))

        def arrive():
            for copy in copies:
                copy.wait_recv()

        return arrive

    def reduce_start(slot, val, bufy):
        bufy[gy] = val
        return share(slot, bufy, gy, ngy, "gy", lambda b, i: b.at[i])

    def reduce_end(slot, first, bufy, bufx):
        first()
        bufx[gx] = total([bufy[j] for j in range(ngy)])
        share(slot + 1, bufx, gx, ngx, "gx", lambda b, i: b.at[i])()
        return total([bufx[j] for j in range(ngx)])

    def gather_start(slot, buf, val):
        buf[REACH, gy] = val
        return share(slot, buf, gy, ngy, "gy", lambda b, i: b.at[REACH, i])

    def gather_next(slot, first, buf):
        first()
        copies = []
        for d in range(-REACH, REACH + 1):
            if d == 0:
                continue
            copy = remote(
                buf.at[REACH], buf.at[REACH - d], cs.at[slot, d + REACH], cr.at[slot, d + REACH], gx + d, gy
            )
            to, frm = inside(gx + d, gy), inside(gx - d, gy)
            pl.when(to)(copy.start)
            copies.append((copy, frm))
            pending.append((copy, to))

        def arrive():
            for copy, frm in copies:
                pl.when(frm)(copy.wait_recv)

        return arrive

    for load in loads[:3]:
        load.wait()
    classes = class_ref[...]
    conduct = jnp.zeros(classes.shape, F32)
    for c in range(table_ref.shape[0]):
        conduct = jnp.where(classes == c, table_ref[c], conduct)
    for x in range(4):
        for y in range(4):
            cut = slice(128 * y, 128 * (y + 1))
            rows = pl.ds(4 * (x % 2), 4)
            kh[2 + x // 2, 2 + y, rows, :] = jnp.broadcast_to(conduct[x : x + 1, cut], (4, 128))
            xp[0, 1 + x // 2, 1 + y, rows, :] = modes_ref[:, x, cut]
            xp[1, 1 + x // 2, 1 + y, rows, :] = dirs_ref[:, x, cut]
    pl.semaphore_wait(barrier, count - 1)
    arrive_k = halo(0, lambda a, b: kh.at[a, b], 2, True)
    arrive_xp = halo(1, lambda a, b: xp.at[:, a, b], 1, False)

    loads[3].wait()
    nl = locked_ref.shape[0]
    for x in range(4):
        for y in range(4):
            cut = slice(128 * y, 128 * (y + 1))
            to = pl.ds(128 * ((x // 2) * 4 + y), 128)
            lst[pl.ds(64 * (x % 2), nl), to] = locked_ref[:, x, cut]
            lst[pl.ds(64 * (x % 2) + nl, 4), to] = modes_ref[:, x, cut]

    own_x = xp[0, 1:3, 1:5]
    own_p = xp[1, 1:3, 1:5]
    x8 = flat(own_x)
    high, low = split(lst[...])
    l_high[...] = high
    l_low[...] = low
    mode_dots = fold_locked(m, dot_split(x8, l_high[...], l_low[...], NT))

    arrive_k()
    arrive_xp()
    own_coef = fine_coef(m, kh[1:5, 1:7])
    image_x = stencil(m, xp[0], own_coef)
    image_x8 = flat(image_x)
    image_dots = fold_locked(m, dot_split(image_x8, l_high[...], l_low[...], NT))
    first = reduce_start(0, jnp.where(m.half0, image_dots, mode_dots), by1)

    wide = fine_coef(m, kh[...])
    in_grid = kh[1:5, 1:7] > 0
    dinv0 = inverse(wide[0], in_grid)
    mid = middle_coef(m, wide)
    dinv1 = inverse(mid[0], in_grid)
    own_mid = [c[1:3, 1:5] for c in mid]
    first_c = gather_start(6, ccg, coarse_pack(m, own_mid))
    image_p = stencil(m, xp[1], own_coef)

    sums = reduce_end(0, first, by1, bx1)
    arrive_c = gather_next(0, first_c, ccg)

    f_of = m.sub % 4
    top = jnp.sum(jnp.where(m.lane == nl + f_of, sums, 0.0), axis=1, keepdims=True)
    norm = jnp.sum(jnp.where(m.lane == 64 + nl + f_of, sums, 0.0), axis=1, keepdims=True)
    rayleigh = top / cells / (norm / cells + EPSILON)
    swapped = lanes(sums, 64)
    image_sum = jnp.where(m.half0, sums, swapped)
    mode_sum = jnp.where(m.half0, swapped, sums)
    j_of = m.lane % 64
    in_use = (j_of < count_ref[0]) & (j_of < nl)
    coupling = jnp.where(in_use, (image_sum - mode_sum * rayleigh) / cells, 0.0)
    coupling = jnp.where(j_of == nl + f_of, rayleigh, coupling)
    residual = image_x - unflat(
        dot_split(spread_locked(m, coupling), l_high[...], l_low[...], NN)
    )

    e0h[2:4, 2:6] = residual * dinv0[1:3, 1:5]
    arrive_e0 = halo(2, lambda a, b: e0h.at[a, b], 2, True)
    arrive_c()
    lines = 2 * ngy
    shift = 4.0 / float(lines * lines)
    faces = []
    for y in range(lines):
        tile = ccg[:, y // 2]
        other = lanes(tile, 64)
        low, high = jnp.where(m.half0, tile, other), jnp.where(m.half0, other, tile)
        row = 4 * (y % 2)
        one = []
        for k in range(6):
            src = low if k < 4 else high
            one.append(jnp.broadcast_to(src[:, row + k % 4 : row + k % 4 + 1], (2 * REACH + 1, 4, 128)))
        faces.append(one)
    z4 = m.z[:4]
    pivots, uppers, diags, dinv2 = [], [], [], []
    for y in range(lines):
        xl, xu, yl, yu, zl, zu = faces[y]
        diag = xl + xu + yl + yu + zl + zu
        known = diag > 0
        main = yl + yu + shift * (xl + xu + zl + zu)
        if y:
            main = main - yl * uppers[y - 1]
        piv = 1.0 / jnp.where(known, main, 1.0)
        pivots.append(piv)
        uppers.append(yu * piv)
        diags.append(diag)
        dinv2.append(inverse(diag, known))
        faces[y][4] = jnp.where(z4 < 4, 0.0, zl)
        faces[y][5] = jnp.where(z4 >= NZ - 4, 0.0, zu)

    arrive_e0()
    e0_wide = e0h[...]
    r1 = e0_wide[1:5, 1:7] * (wide[0] * (1.0 / OMEGA)) - stencil(m, e0_wide, wide)
    r1 = pair_z(m, pair_y(pair_x(r1)))
    e1_near = r1 * dinv1
    e1h[2:4, 2:6] = e1_near[1:3, 1:5]
    arrive_e1 = halo(3, lambda a, b: e1h.at[a, b], 2, True)
    r2 = r1[1:3, 1:5] - middle_stencil(m, e1_near, own_mid)
    r2 = r2[0] + r2[1]
    r2 = jnp.where(m.par0, r2[0] + r2[1], r2[2] + r2[3])
    first_r = gather_start(7, r2g, pair_z2(m, r2))
    gather_next(1, first_r, r2g)()

    source = [r2g[:, y // 2, 4 * (y % 2) : 4 * (y % 2) + 4] for y in range(lines)]
    held = []
    for y in range(lines):
        right = source[y] if y == 0 else source[y] + faces[y][2] * held[y - 1]
        held.append(right * pivots[y])
    for y in range(lines - 2, -1, -1):
        held[y] = held[y] + uppers[y] * held[y + 1]
    for sweep in range(1, SWEEPS):
        nxt = []
        for y in range(lines):
            cut = slice(sweep, 2 * REACH + 1 - sweep)
            c = [f[cut] for f in faces[y]]
            u = held[y]
            mid_u = u[1:-1]
            beside = c[0] * u[:-2] + c[1] * u[2:]
            if y:
                beside = beside + c[2] * held[y - 1][1:-1]
            if y < lines - 1:
                beside = beside + c[3] * held[y + 1][1:-1]
            beside = beside + c[4] * lanes(mid_u, 4) + c[5] * lanes(mid_u, -4)
            off = source[y][cut] - (diags[y][cut] * mid_u - beside)
            nxt.append(mid_u + dinv2[y][cut] * off)
        held = nxt
    for y in range(lines):
        e2s[1 + y] = held[y]
    near = e2s[pl.ds(2 * gy, 4)]
    near = jnp.concatenate([near, near], axis=2)

    arrive_e1()
    e1_wide = e1h[...]
    e1_wide = jnp.stack(
        [jnp.stack([e1_wide[a, b] + near[b // 2, a // 2] for b in range(8)]) for a in range(6)]
    )
    e1 = e1_wide[1:5, 1:7] + e1h[1:5, 1:7] - dinv1 * middle_stencil(m, e1_wide, mid)
    e0 = e0_wide[1:5, 1:7] + e1
    precond = e0[1:3, 1:5] + e0_wide[2:4, 2:6] - dinv0[1:3, 1:5] * stencil(m, e0, own_coef)

    precond8 = flat(precond)
    dots = fold_locked(m, dot_split(precond8, l_high[...], l_low[...], NT))
    sums = reduce_end(2, reduce_start(2, dots, by2), by2, bx2)
    corr = jnp.where(in_use, sums / cells, 0.0)
    corr_ref[...] = corr[:ACTIVE, : corr_ref.shape[1]]
    projected8 = precond8 - dot_split(spread_locked(m, corr), l_high[...], l_low[...], NN)
    wh[1:3, 1:5] = unflat(projected8)
    halo(4, lambda a, b: wh.at[a, b], 1, False)()
    image_w = stencil(m, wh[...], own_coef)

    fields = jnp.concatenate(
        [x8, projected8, flat(own_p), image_x8, flat(image_w), flat(image_p)], axis=0
    )
    f_high, f_low = split(fields)
    grams = dot_split(fields, f_high, f_low, NT)
    mass = grams[:24, :24]
    stiff = 0.5 * (grams[:24, 24:] + grams[24:, :24])
    both = jnp.concatenate([mass, jnp.zeros((24, 8), F32), stiff, jnp.zeros((24, 72), F32)], axis=1)
    row, col = iota((24, 128), 0), iota((24, 128), 1)
    both = jnp.where((row // 4) % 2 == (col // 4) % 2, both, 0.0)
    both = both + jnp.concatenate([subs(both[8 * i : 8 * i + 8], 4) for i in range(3)], axis=0)
    both = both + lanes(both, -4)
    sums = reduce_end(4, reduce_start(4, both, by3), by3, bx3) / cells

    real = row % 8 < 4
    table = jnp.where(real & (col < 64) & (col % 8 < 4), sums, 0.0)
    table = jnp.where(real & (col == row + 64), 1.0, table)
    pivots_at = [8 * g + f for g in range(3) for f in range(4)]

    def eliminate(work, order, rows):
        for k in order:
            pivot = work[k : k + 1, k : k + 1]
            scale = lax.rsqrt(pivot)
            line = work[k : k + 1, :] * scale
            factor = jnp.where(rows > k, work[:, k : k + 1] * scale, 0.0)
            work = jnp.where(rows == k, line, work - factor * line)
        return work

    work = eliminate(table, pivots_at, row)
    half = jnp.where(col < 24, lanes(work, -32), 0.0)
    linv = jnp.where(col < 24, lanes(work, -64), 0.0)
    reduced = 0.5 * (nt(half, linv) + nt(linv, half))
    reduced = jnp.concatenate([reduced, jnp.zeros((24, 104), F32)], axis=1)
    spectral = jnp.sum(jnp.where(row == col, reduced, 0.0), keepdims=True)
    raised = jnp.where((row == col) & real, spectral, 0.0) - reduced
    full = jnp.concatenate([raised, jnp.zeros((104, 128), F32)], axis=0)
    reduced_full = jnp.concatenate([reduced, jnp.zeros((104, 128), F32)], axis=0)
    basis = jnp.where(m.par0, raised[:8], 0.0)
    for step in range(RITZ - 1):
        basis = nn(basis, full)
    square = nt(basis, basis)
    small = jnp.concatenate([square, jnp.zeros((8, 120), F32)], axis=1) + lanes(basis, 32)
    small = eliminate(small, range(4), m.sub)
    basis = jnp.where((m.lane < 24) & m.par0, lanes(small, -32), 0.0)
    ritz = jnp.sum(basis * nn(basis, reduced_full), axis=1, keepdims=True)
    for k in range(ACTIVE):
        ritz_ref[k] = ritz[k, 0]
    linv_full = jnp.concatenate([linv, jnp.zeros((104, 128), F32)], axis=0)
    coef = nn(basis, linv_full)
    coef = coef + lanes(coef, 4)
    coef = coef + subs(coef, 4)
    coef = jnp.where(m.par0 == ((m.lane // 4) % 2 == 0), coef, 0.0)[:, :24]
    later = jnp.where(iota((8, 24), 1) >= 8, coef, 0.0)
    pad = jnp.zeros((16, 24), F32)
    mixed = dot_split(
        jnp.concatenate([jnp.concatenate([coef, later], axis=0), pad], axis=1), f_high, f_low, NN
    )
    modes8, dirs8 = mixed[:8], mixed[8:]
    for x in range(4):
        for y in range(4):
            cut = slice(128 * y, 128 * (y + 1))
            frm = slice(128 * ((x // 2) * 4 + y), 128 * ((x // 2) * 4 + y + 1))
            rows = slice(4 * (x % 2), 4 * (x % 2) + 4)
            new_modes_ref[:, x, cut] = modes8[rows, frm]
            new_dirs_ref[:, x, cut] = dirs8[rows, frm]

    for copy, to in pending:
        if to is None:
            copy.wait_send()
        else:
            pl.when(to)(copy.wait_send)


def on_device(ngx, ngy, modes, directions, locked, perm_class, perm_table, locked_count):
    vmem = pl.BlockSpec(memory_space=pltpu.VMEM)
    smem = pl.BlockSpec(memory_space=pltpu.SMEM)
    dma = pltpu.SemaphoreType.DMA
    wide = 2 * REACH + 1
    hbm = pl.BlockSpec(memory_space=pltpu.HBM)
    new_modes, new_dirs, ritz, corr = pl.pallas_call(
        functools.partial(kernel, ngx, ngy),
        out_shape=(
            jax.ShapeDtypeStruct(modes.shape, F32),
            jax.ShapeDtypeStruct(modes.shape, F32),
            jax.ShapeDtypeStruct((ACTIVE,), F32),
            jax.ShapeDtypeStruct((ACTIVE, locked.shape[0]), F32),
        ),
        in_specs=[hbm, hbm, hbm, hbm, smem, smem],
        out_specs=(vmem, vmem, smem, vmem),
        scratch_shapes=[
            pltpu.VMEM((6, 8, 8, 128), F32),
            pltpu.VMEM((2, 4, 6, 8, 128), F32),
            pltpu.VMEM((6, 8, 8, 128), F32),
            pltpu.VMEM((6, 8, 8, 128), F32),
            pltpu.VMEM((4, 6, 8, 128), F32),
            pltpu.VMEM((wide, ngy, 8, 128), F32),
            pltpu.VMEM((wide, ngy, 8, 128), F32),
            pltpu.VMEM((2 * ngy + 2, 3, 4, 128), F32),
            pltpu.VMEM((128, 1024), F32),
            pltpu.VMEM((128, 1024), BF16),
            pltpu.VMEM((128, 1024), BF16),
            pltpu.VMEM(modes.shape, F32),
            pltpu.VMEM(directions.shape, F32),
            pltpu.VMEM(locked.shape, F32),
            pltpu.VMEM(perm_class.shape, jnp.int32),
            dma((4,)),
            pltpu.VMEM((ngy, 8, 128), F32),
            pltpu.VMEM((ngx, 8, 128), F32),
            pltpu.VMEM((ngy, 8, 128), F32),
            pltpu.VMEM((ngx, 8, 128), F32),
            pltpu.VMEM((ngy, 24, 128), F32),
            pltpu.VMEM((ngx, 24, 128), F32),
            dma((5, 9)),
            dma((5, 9)),
            dma((8, max(ngx, ngy))),
            dma((8, max(ngx, ngy))),
            dma((2, wide)),
            dma((2, wide)),
        ],
        compiler_params=pltpu.CompilerParams(
            collective_id=0, has_side_effects=True, vmem_limit_bytes=64 * 1024 * 1024 - 65536
        ),
    )(modes, directions, locked, perm_class, perm_table, locked_count)
    return new_modes, new_dirs, ritz, corr.T


def solution(mesh):
    placed = (
        P(None, "gx", "gy"),
        P(None, "gx", "gy"),
        P(None, "gx", "gy"),
        P("gx", "gy"),
        P(),
        P(),
    )
    return jax.shard_map(
        functools.partial(on_device, mesh.shape["gx"], mesh.shape["gy"]),
        mesh=mesh,
        in_specs=placed,
        out_specs=(P(None, "gx", "gy"), P(None, "gx", "gy"), P(), P()),
        check_vma=False,
    )
```

```python
import functools

import jax
import jax.numpy as jnp
from jax import lax
from jax.experimental import pallas as pl
from jax.experimental.pallas import tpu as pltpu
from jax.sharding import PartitionSpec as P

NZ = 64
ACTIVE = 4
SWEEPS = 3
RITZ = 3
OMEGA = 0.6
EPSILON = 1e-06
PRECISE = lax.Precision.HIGHEST
F32 = jnp.float32
REACH = SWEEPS


def iota(shape, dim):
    return lax.broadcasted_iota(jnp.int32, shape, dim)


def nt(a, b):
    return lax.dot_general(a, b, (((1,), (1,)), ((), ())), precision=PRECISE, preferred_element_type=F32)


def nn(a, b):
    return lax.dot_general(a, b, (((1,), (0,)), ((), ())), precision=PRECISE, preferred_element_type=F32)


def lanes(u, by):
    return pltpu.roll(u, by % 128, u.ndim - 1)


def subs(u, by):
    return pltpu.roll(u, by % 8, u.ndim - 2)


def face_value(a, b):
    both = (a > 0) & (b > 0)
    return jnp.where(both, 2.0 * a * b / jnp.where(both, a + b, 1.0), 2.0 * (a + b))


BF16 = jnp.bfloat16


def split(a):
    high = a.astype(BF16)
    return high, (a - high.astype(F32)).astype(BF16)


def dot_split(a, b_high, b_low, dims):
    rows = a.shape[0]
    high = a.astype(BF16).astype(F32)
    stack = jnp.concatenate([high, a - high], axis=0).astype(BF16)
    dims = (dims, ((), ()))
    one = lax.dot_general(stack, b_high, dims, preferred_element_type=F32)
    two = lax.dot_general(high.astype(BF16), b_low, dims, preferred_element_type=F32)
    return one[:rows] + (one[rows:] + two)


NT = ((1,), (1,))
NN = ((1,), (0,))


class Marks:
    def __init__(self):
        lane = iota((8, 128), 1)
        sub = iota((8, 128), 0)
        self.lane = lane
        self.sub = sub
        self.z = lane % NZ
        self.half0 = lane < 64
        self.par0 = sub < 4
        self.even = lane % 2 == 0
        self.quad = lane % 4 < 2


def neighbours(m, u):
    inner = u[1:-1, 1:-1]
    zl = jnp.where(m.z == 0, 0.0, lanes(inner, 1))
    zu = jnp.where(m.z == NZ - 1, 0.0, lanes(inner, -1))
    flip = lanes(u[1:-1], 64)
    yl = jnp.where(m.half0, flip[:, :-2], flip[:, 1:-1])
    yu = jnp.where(m.half0, flip[:, 1:-1], flip[:, 2:])
    turn = subs(u[:, 1:-1], 4)
    xl = jnp.where(m.par0, turn[:-2], turn[1:-1])
    xu = jnp.where(m.par0, turn[1:-1], turn[2:])
    return xl, xu, yl, yu, zl, zu


def total(parts):
    out = parts[0]
    for part in parts[1:]:
        out = out + part
    return out


def fine_coef(m, k):
    inner = k[1:-1, 1:-1]
    faces = [face_value(near, inner) for near in neighbours(m, k)]
    return [total(faces)] + faces


def stencil(m, u, coef):
    near = neighbours(m, u)
    return coef[0] * u[1:-1, 1:-1] - total([c * v for c, v in zip(coef[1:], near)])


def inverse(diag, inside):
    return jnp.where(inside, OMEGA / jnp.where(inside, diag, 1.0), 0.0)


def pair_x(u):
    return u + subs(u, 4)


def pair_y(u):
    return u + lanes(u, 64)


def pair_z(m, u):
    return u + jnp.where(m.even, lanes(u, -1), lanes(u, 1))


def pair_z2(m, u):
    return u + jnp.where(m.quad, lanes(u, -2), lanes(u, 2))


def middle_coef(m, c):
    xl = pair_z(m, pair_y(jnp.where(m.par0, c[1], subs(c[1], 4))))
    xu = pair_z(m, pair_y(jnp.where(m.par0, subs(c[2], 4), c[2])))
    yl = pair_z(m, pair_x(jnp.where(m.half0, c[3], lanes(c[3], 64))))
    yu = pair_z(m, pair_x(jnp.where(m.half0, lanes(c[4], 64), c[4])))
    zl = pair_y(pair_x(jnp.where(m.even, c[5], lanes(c[5], 1))))
    zu = pair_y(pair_x(jnp.where(m.even, lanes(c[6], -1), c[6])))
    faces = [xl, xu, yl, yu, zl, zu]
    return [total(faces)] + faces


def middle_stencil(m, u, coef):
    inner = u[1:-1, 1:-1]
    zl = jnp.where(m.z < 2, 0.0, lanes(inner, 2))
    zu = jnp.where(m.z >= NZ - 2, 0.0, lanes(inner, -2))
    near = [u[:-2, 1:-1], u[2:, 1:-1], u[1:-1, :-2], u[1:-1, 2:], zl, zu]
    return coef[0] * inner - total([c * v for c, v in zip(coef[1:], near)])


def coarse_pack(m, mid):
    _, xl, xu, yl, yu, zl, zu = mid
    out = jnp.zeros((8, 128), F32)
    for q in range(2):
        a, b = 2 * q, 2 * q + 1
        faces = [
            pair_z2(m, xl[0, a] + xl[0, b]),
            pair_z2(m, xu[1, a] + xu[1, b]),
            pair_z2(m, yl[0, a] + yl[1, a]),
            pair_z2(m, yu[0, b] + yu[1, b]),
        ]
        low = zl[0, a] + zl[0, b] + zl[1, a] + zl[1, b]
        high = zu[0, a] + zu[0, b] + zu[1, a] + zu[1, b]
        faces.append(jnp.where(m.quad, low, lanes(low, 2)))
        faces.append(jnp.where(m.quad, lanes(high, -2), high))
        for k in range(6):
            spot = (m.sub == 4 * q + k % 4) & (m.half0 if k < 4 else ~m.half0)
            out = jnp.where(spot, faces[k], out)
    return out


def flat(u):
    return jnp.concatenate([u[x, y] for x in range(2) for y in range(4)], axis=1)


def unflat(u):
    tiles = [u[:, 128 * i : 128 * (i + 1)] for i in range(8)]
    return jnp.stack([jnp.stack(tiles[:4]), jnp.stack(tiles[4:])])


def fold_locked(m, g):
    g = jnp.where(m.par0 == m.half0, g, 0.0)
    return pair_y(pair_x(g))


def spread_locked(m, c):
    return jnp.where(m.par0 == m.half0, c, 0.0)


def kernel(
    ngx,
    ngy,
    modes_hbm,
    dirs_hbm,
    locked_hbm,
    class_hbm,
    table_ref,
    count_ref,
    sums_ref,
    trial_ref,
    corr_ref,
    kh,
    xp,
    e0h,
    e1h,
    wh,
    ccg,
    r2g,
    e2s,
    lst,
    l_high,
    l_low,
    modes_ref,
    dirs_ref,
    locked_ref,
    class_ref,
    ins,
    by1,
    bx1,
    by2,
    bx2,
    by3,
    bx3,
    hs,
    hr,
    rs,
    rr,
    cs,
    cr,
):
    loads = [
        pltpu.make_async_copy(src, dst, ins.at[i])
        for i, (src, dst) in enumerate(
            [(class_hbm, class_ref), (modes_hbm, modes_ref), (dirs_hbm, dirs_ref), (locked_hbm, locked_ref)]
        )
    ]
    for load in loads:
        load.start()
    m = Marks()
    gx, gy = lax.axis_index("gx"), lax.axis_index("gy")
    count = ngx * ngy
    cells = float(4 * 512 * count)
    pending = []

    for buf in (kh, xp, e0h, e1h, wh, ccg, r2g, e2s):
        buf[...] = jnp.zeros(buf.shape, F32)

    barrier = pltpu.get_barrier_semaphore()

    def greet(tx, ty):
        pl.semaphore_signal(barrier, inc=1, device_id=(tx, ty), device_id_type=pl.DeviceIdType.MESH)

    for i in range(1, ngx):
        greet(lax.rem(gx + i, ngx), gy)
    for i in range(1, ngy):
        greet(gx, lax.rem(gy + i, ngy))
    for dx in (-1, 1):
        for dy in (-1, 1):
            pl.when(
                (gx + dx >= 0) & (gx + dx < ngx) & (gy + dy >= 0) & (gy + dy < ngy)
            )(functools.partial(greet, gx + dx, gy + dy))
    beside_x = jnp.where(gx > 0, 1, 0) + jnp.where(gx < ngx - 1, 1, 0)
    beside_y = jnp.where(gy > 0, 1, 0) + jnp.where(gy < ngy - 1, 1, 0)
    greeted = ngx + ngy - 2 + beside_x * beside_y

    def remote(src, dst, send, recv, tx, ty):
        return pltpu.make_async_remote_copy(
            src_ref=src, dst_ref=dst, send_sem=send, recv_sem=recv, device_id=(tx, ty),
            device_id_type=pl.DeviceIdType.MESH,
        )

    def inside(tx, ty):
        return (tx >= 0) & (tx < ngx) & (ty >= 0) & (ty < ngy)

    def halo(slot, view, w, corners):
        def span(d, n):
            if d > 0:
                return pl.ds(n, w), pl.ds(0, w)
            if d < 0:
                return pl.ds(w, w), pl.ds(w + n, w)
            return pl.ds(w, n), pl.ds(w, n)

        copies = []
        for dx in (-1, 0, 1):
            for dy in (-1, 0, 1):
                if (dx, dy) == (0, 0) or (dx and dy and not corners):
                    continue
                (sx, tx), (sy, ty) = span(dx, 2), span(dy, 4)
                n = (dx + 1) * 3 + dy + 1
                copy = remote(view(sx, sy), view(tx, ty), hs.at[slot, n], hr.at[slot, n], gx + dx, gy + dy)
                to, frm = inside(gx + dx, gy + dy), inside(gx - dx, gy - dy)
                pl.when(to)(copy.start)
                copies.append((copy, frm))
                pending.append((copy, to))

        def arrive():
            for copy, frm in copies:
                pl.when(frm)(copy.wait_recv)

        return arrive

    def share(slot, buf, mine, n, axis, view):
        copies = []
        for i in range(1, n):
            to, frm = lax.rem(mine + i, n), lax.rem(mine + n - i, n)
            where = (gx, to) if axis == "gy" else (to, gy)
            back = (gx, frm) if axis == "gy" else (frm, gy)
            copy = remote(view(buf, mine), view(buf, mine), rs.at[slot, i], rr.at[slot, i], *where)
            copy.start()
            pending.append((copy, None))
            copies.append(remote(view(buf, frm), view(buf, frm), rs.at[slot, i], rr.at[slot, i], *back))

        def arrive():
            for copy in copies:
                copy.wait_recv()

        return arrive

    def reduce_start(slot, val, bufy):
        bufy[gy] = val
        return share(slot, bufy, gy, ngy, "gy", lambda b, i: b.at[i])

    def reduce_next(slot, first, bufy, bufx):
        first()
        bufx[gx] = total([bufy[j] for j in range(ngy)])
        return share(slot + 1, bufx, gx, ngx, "gx", lambda b, i: b.at[i])

    def reduce_end(slot, first, bufy, bufx):
        reduce_next(slot, first, bufy, bufx)()
        return total([bufx[j] for j in range(ngx)])

    def gather_start(slot, buf, val):
        buf[REACH, gy] = val
        return share(slot, buf, gy, ngy, "gy", lambda b, i: b.at[REACH, i])

    def gather_next(slot, first, buf):
        first()
        copies = []
        for d in range(-REACH, REACH + 1):
            if d == 0:
                continue
            copy = remote(
                buf.at[REACH], buf.at[REACH - d], cs.at[slot, d + REACH], cr.at[slot, d + REACH], gx + d, gy
            )
            to, frm = inside(gx + d, gy), inside(gx - d, gy)
            pl.when(to)(copy.start)
            copies.append((copy, frm))
            pending.append((copy, to))

        def arrive():
            for copy, frm in copies:
                pl.when(frm)(copy.wait_recv)

        return arrive

    for load in loads[:3]:
        load.wait()
    classes = class_ref[...]
    conduct = jnp.zeros(classes.shape, F32)
    for c in range(table_ref.shape[0]):
        conduct = jnp.where(classes == c, table_ref[c], conduct)
    for x in range(4):
        for y in range(4):
            cut = slice(128 * y, 128 * (y + 1))
            rows = pl.ds(4 * (x % 2), 4)
            kh[2 + x // 2, 2 + y, rows, :] = jnp.broadcast_to(conduct[x : x + 1, cut], (4, 128))
            xp[0, 1 + x // 2, 1 + y, rows, :] = modes_ref[:, x, cut]
            xp[1, 1 + x // 2, 1 + y, rows, :] = dirs_ref[:, x, cut]
    pl.semaphore_wait(barrier, greeted)
    arrive_k = halo(0, lambda a, b: kh.at[a, b], 2, True)
    arrive_xp = halo(1, lambda a, b: xp.at[:, a, b], 1, False)

    loads[3].wait()
    nl = locked_ref.shape[0]
    for x in range(4):
        for y in range(4):
            cut = slice(128 * y, 128 * (y + 1))
            to = pl.ds(128 * ((x // 2) * 4 + y), 128)
            lst[pl.ds(64 * (x % 2), nl), to] = locked_ref[:, x, cut]
            lst[pl.ds(64 * (x % 2) + nl, 4), to] = modes_ref[:, x, cut]

    own_x = xp[0, 1:3, 1:5]
    own_p = xp[1, 1:3, 1:5]
    x8 = flat(own_x)
    high, low = split(lst[...])
    l_high[...] = high
    l_low[...] = low
    mode_dots = fold_locked(m, dot_split(x8, l_high[...], l_low[...], NT))

    arrive_k()
    arrive_xp()
    own_coef = fine_coef(m, kh[1:5, 1:7])
    image_x = stencil(m, xp[0], own_coef)
    image_x8 = flat(image_x)
    image_dots = fold_locked(m, dot_split(image_x8, l_high[...], l_low[...], NT))
    first = reduce_start(0, jnp.where(m.half0, image_dots, mode_dots), by1)

    wide = fine_coef(m, kh[...])
    in_grid = kh[1:5, 1:7] > 0
    dinv0 = inverse(wide[0], in_grid)
    second = reduce_next(0, first, by1, bx1)
    mid = middle_coef(m, wide)
    dinv1 = inverse(mid[0], in_grid)
    own_mid = [c[1:3, 1:5] for c in mid]
    first_c = gather_start(6, ccg, coarse_pack(m, own_mid))
    image_p = stencil(m, xp[1], own_coef)
    second()
    sums = total([bx1[j] for j in range(ngx)])

    f_of = m.sub % 4
    top = jnp.sum(jnp.where(m.lane == nl + f_of, sums, 0.0), axis=1, keepdims=True)
    norm = jnp.sum(jnp.where(m.lane == 64 + nl + f_of, sums, 0.0), axis=1, keepdims=True)
    rayleigh = top / cells / (norm / cells + EPSILON)
    swapped = lanes(sums, 64)
    image_sum = jnp.where(m.half0, sums, swapped)
    mode_sum = jnp.where(m.half0, swapped, sums)
    j_of = m.lane % 64
    in_use = (j_of < count_ref[0]) & (j_of < nl)
    coupling = jnp.where(in_use, (image_sum - mode_sum * rayleigh) / cells, 0.0)
    coupling = jnp.where(j_of == nl + f_of, rayleigh, coupling)
    residual = image_x - unflat(
        dot_split(spread_locked(m, coupling), l_high[...], l_low[...], NN)
    )

    e0h[2:4, 2:6] = residual * dinv0[1:3, 1:5]
    arrive_e0 = halo(2, lambda a, b: e0h.at[a, b], 2, True)
    arrive_c = gather_next(0, first_c, ccg)
    arrive_e0()
    e0_wide = e0h[...]
    r1 = e0_wide[1:5, 1:7] * (wide[0] * (1.0 / OMEGA)) - stencil(m, e0_wide, wide)
    r1 = pair_z(m, pair_y(pair_x(r1)))
    e1_near = r1 * dinv1
    e1h[2:4, 2:6] = e1_near[1:3, 1:5]
    arrive_e1 = halo(3, lambda a, b: e1h.at[a, b], 2, True)
    r2 = r1[1:3, 1:5] - middle_stencil(m, e1_near, own_mid)
    r2 = r2[0] + r2[1]
    r2 = jnp.where(m.par0, r2[0] + r2[1], r2[2] + r2[3])
    first_r = gather_start(7, r2g, pair_z2(m, r2))
    arrive_c()
    lines = 2 * ngy
    shift = 4.0 / float(lines * lines)
    faces = []
    for y in range(lines):
        tile = ccg[:, y // 2]
        other = lanes(tile, 64)
        low, high = jnp.where(m.half0, tile, other), jnp.where(m.half0, other, tile)
        row = 4 * (y % 2)
        one = []
        for k in range(6):
            src = low if k < 4 else high
            one.append(jnp.broadcast_to(src[:, row + k % 4 : row + k % 4 + 1], (2 * REACH + 1, 4, 128)))
        faces.append(one)
    z4 = m.z[:4]
    pivots, uppers, diags, dinv2 = [], [], [], []
    for y in range(lines):
        xl, xu, yl, yu, zl, zu = faces[y]
        diag = xl + xu + yl + yu + zl + zu
        known = diag > 0
        main = yl + yu + shift * (xl + xu + zl + zu)
        if y:
            main = main - yl * uppers[y - 1]
        piv = 1.0 / jnp.where(known, main, 1.0)
        pivots.append(piv)
        uppers.append(yu * piv)
        diags.append(diag)
        dinv2.append(inverse(diag, known))
        faces[y][4] = jnp.where(z4 < 4, 0.0, zl)
        faces[y][5] = jnp.where(z4 >= NZ - 4, 0.0, zu)

    gather_next(1, first_r, r2g)()

    source = [r2g[:, y // 2, 4 * (y % 2) : 4 * (y % 2) + 4] for y in range(lines)]
    held = []
    for y in range(lines):
        right = source[y] if y == 0 else source[y] + faces[y][2] * held[y - 1]
        held.append(right * pivots[y])
    for y in range(lines - 2, -1, -1):
        held[y] = held[y] + uppers[y] * held[y + 1]
    for sweep in range(1, SWEEPS):
        nxt = []
        for y in range(lines):
            cut = slice(sweep, 2 * REACH + 1 - sweep)
            c = [f[cut] for f in faces[y]]
            u = held[y]
            mid_u = u[1:-1]
            beside = c[0] * u[:-2] + c[1] * u[2:]
            if y:
                beside = beside + c[2] * held[y - 1][1:-1]
            if y < lines - 1:
                beside = beside + c[3] * held[y + 1][1:-1]
            beside = beside + c[4] * lanes(mid_u, 4) + c[5] * lanes(mid_u, -4)
            off = source[y][cut] - (diags[y][cut] * mid_u - beside)
            nxt.append(mid_u + dinv2[y][cut] * off)
        held = nxt
    for y in range(lines):
        e2s[1 + y] = held[y]
    near = e2s[pl.ds(2 * gy, 4)]
    near = jnp.concatenate([near, near], axis=2)

    arrive_e1()
    e1_wide = e1h[...]
    e1_wide = jnp.stack(
        [jnp.stack([e1_wide[a, b] + near[b // 2, a // 2] for b in range(8)]) for a in range(6)]
    )
    e1 = e1_wide[1:5, 1:7] + e1h[1:5, 1:7] - dinv1 * middle_stencil(m, e1_wide, mid)
    e0 = e0_wide[1:5, 1:7] + e1
    precond = e0[1:3, 1:5] + e0_wide[2:4, 2:6] - dinv0[1:3, 1:5] * stencil(m, e0, own_coef)

    precond8 = flat(precond)
    dots = fold_locked(m, dot_split(precond8, l_high[...], l_low[...], NT))
    sums = reduce_end(2, reduce_start(2, dots, by2), by2, bx2)
    corr = jnp.where(in_use, sums / cells, 0.0)
    corr_ref[...] = corr[:ACTIVE, : corr_ref.shape[1]]
    projected8 = precond8 - dot_split(spread_locked(m, corr), l_high[...], l_low[...], NN)
    wh[1:3, 1:5] = unflat(projected8)
    halo(4, lambda a, b: wh.at[a, b], 1, False)()
    image_w = stencil(m, wh[...], own_coef)

    fields = jnp.concatenate(
        [x8, projected8, flat(own_p), image_x8, flat(image_w), flat(image_p)], axis=0
    )
    f_high, f_low = split(fields)
    grams = dot_split(fields, f_high, f_low, NT)
    mass = grams[:24, :24]
    stiff = 0.5 * (grams[:24, 24:] + grams[24:, :24])
    both = jnp.concatenate([mass, jnp.zeros((24, 8), F32), stiff, jnp.zeros((24, 72), F32)], axis=1)
    row, col = iota((24, 128), 0), iota((24, 128), 1)
    both = jnp.where((row // 4) % 2 == (col // 4) % 2, both, 0.0)
    both = both + jnp.concatenate([subs(both[8 * i : 8 * i + 8], 4) for i in range(3)], axis=0)
    both = both + lanes(both, -4)
    trial_ref[...] = fields[:24]
    sums_ref[...] = reduce_end(4, reduce_start(4, both, by3), by3, bx3) / cells

    for copy, to in pending:
        if to is None:
            copy.wait_send()
        else:
            pl.when(to)(copy.wait_send)


def finish(
    sums_hbm, trial_hbm, corr_hbm, new_modes_hbm, new_dirs_hbm, ritz_ref, corr_out,
    sums_ref, trial_ref, corr_ref, new_modes_ref, new_dirs_ref, sems,
):
    loads = [
        pltpu.make_async_copy(sums_hbm, sums_ref, sems.at[0]),
        pltpu.make_async_copy(trial_hbm, trial_ref, sems.at[1]),
        pltpu.make_async_copy(corr_hbm, corr_ref, sems.at[2]),
    ]
    for load in loads:
        load.start()
    m = Marks()
    row, col = iota((24, 128), 0), iota((24, 128), 1)
    for load in loads:
        load.wait()
    store_corr = pltpu.make_async_copy(corr_ref, corr_out, sems.at[3])
    store_corr.start()
    sums = sums_ref[...]
    real = row % 8 < 4
    table = jnp.where(real & (col < 64) & (col % 8 < 4), sums, 0.0)
    table = jnp.where(real & (col == row + 64), 1.0, table)
    pivots_at = [8 * g + f for g in range(3) for f in range(4)]

    def eliminate(work, order, rows):
        for k in order:
            pivot = work[k : k + 1, k : k + 1]
            scale = lax.rsqrt(pivot)
            line = work[k : k + 1, :] * scale
            factor = jnp.where(rows > k, work[:, k : k + 1] * scale, 0.0)
            work = jnp.where(rows == k, line, work - factor * line)
        return work

    work = eliminate(table, pivots_at, row)
    half = jnp.where(col < 24, lanes(work, -32), 0.0)
    linv = jnp.where(col < 24, lanes(work, -64), 0.0)
    reduced = 0.5 * (nt(half, linv) + nt(linv, half))
    reduced = jnp.concatenate([reduced, jnp.zeros((24, 104), F32)], axis=1)
    spectral = jnp.sum(jnp.where(row == col, reduced, 0.0), keepdims=True)
    raised = jnp.where((row == col) & real, spectral, 0.0) - reduced
    full = jnp.concatenate([raised, jnp.zeros((104, 128), F32)], axis=0)
    reduced_full = jnp.concatenate([reduced, jnp.zeros((104, 128), F32)], axis=0)
    basis = jnp.where(m.par0, raised[:8], 0.0)
    for step in range(RITZ - 1):
        basis = nn(basis, full)
    square = nt(basis, basis)
    small = jnp.concatenate([square, jnp.zeros((8, 120), F32)], axis=1) + lanes(basis, 32)
    small = eliminate(small, range(4), m.sub)
    basis = jnp.where((m.lane < 24) & m.par0, lanes(small, -32), 0.0)
    ritz = jnp.sum(basis * nn(basis, reduced_full), axis=1, keepdims=True)
    for k in range(ACTIVE):
        ritz_ref[k] = ritz[k, 0]
    linv_full = jnp.concatenate([linv, jnp.zeros((104, 128), F32)], axis=0)
    coef = nn(basis, linv_full)
    coef = coef + lanes(coef, 4)
    coef = coef + subs(coef, 4)
    coef = jnp.where(m.par0 == ((m.lane // 4) % 2 == 0), coef, 0.0)[:, :24]
    f_high, f_low = split(trial_ref[...])
    later = jnp.where(iota((8, 24), 1) >= 8, coef, 0.0)
    mixed = dot_split(jnp.concatenate([coef, later], axis=0), f_high, f_low, NN)
    modes8, dirs8 = mixed[:8], mixed[8:]
    for x in range(4):
        for y in range(4):
            cut = slice(128 * y, 128 * (y + 1))
            frm = slice(128 * ((x // 2) * 4 + y), 128 * ((x // 2) * 4 + y + 1))
            rows = slice(4 * (x % 2), 4 * (x % 2) + 4)
            new_modes_ref[:, x, cut] = modes8[rows, frm]
            new_dirs_ref[:, x, cut] = dirs8[rows, frm]
    stores = [
        pltpu.make_async_copy(new_modes_ref, new_modes_hbm, sems.at[4]),
        pltpu.make_async_copy(new_dirs_ref, new_dirs_hbm, sems.at[5]),
    ]
    for store in stores:
        store.start()
    for store in stores + [store_corr]:
        store.wait()


def on_device(ngx, ngy, modes, directions, locked, perm_class, perm_table, locked_count):
    vmem = pl.BlockSpec(memory_space=pltpu.VMEM)
    smem = pl.BlockSpec(memory_space=pltpu.SMEM)
    dma = pltpu.SemaphoreType.DMA
    wide = 2 * REACH + 1
    hbm = pl.BlockSpec(memory_space=pltpu.HBM)
    limit = 64 * 1024 * 1024 - 65536
    sums, trial, corr = pl.pallas_call(
        functools.partial(kernel, ngx, ngy),
        out_shape=(
            jax.ShapeDtypeStruct((24, 128), F32),
            jax.ShapeDtypeStruct((24, 1024), F32),
            jax.ShapeDtypeStruct((ACTIVE, locked.shape[0]), F32),
        ),
        in_specs=[hbm, hbm, hbm, hbm, smem, smem],
        out_specs=(vmem, vmem, vmem),
        scratch_shapes=[
            pltpu.VMEM((6, 8, 8, 128), F32),
            pltpu.VMEM((2, 4, 6, 8, 128), F32),
            pltpu.VMEM((6, 8, 8, 128), F32),
            pltpu.VMEM((6, 8, 8, 128), F32),
            pltpu.VMEM((4, 6, 8, 128), F32),
            pltpu.VMEM((wide, ngy, 8, 128), F32),
            pltpu.VMEM((wide, ngy, 8, 128), F32),
            pltpu.VMEM((2 * ngy + 2, 3, 4, 128), F32),
            pltpu.VMEM((128, 1024), F32),
            pltpu.VMEM((128, 1024), BF16),
            pltpu.VMEM((128, 1024), BF16),
            pltpu.VMEM(modes.shape, F32),
            pltpu.VMEM(directions.shape, F32),
            pltpu.VMEM(locked.shape, F32),
            pltpu.VMEM(perm_class.shape, jnp.int32),
            dma((4,)),
            pltpu.VMEM((ngy, 8, 128), F32),
            pltpu.VMEM((ngx, 8, 128), F32),
            pltpu.VMEM((ngy, 8, 128), F32),
            pltpu.VMEM((ngx, 8, 128), F32),
            pltpu.VMEM((ngy, 24, 128), F32),
            pltpu.VMEM((ngx, 24, 128), F32),
            dma((5, 9)),
            dma((5, 9)),
            dma((8, max(ngx, ngy))),
            dma((8, max(ngx, ngy))),
            dma((2, wide)),
            dma((2, wide)),
        ],
        compiler_params=pltpu.CompilerParams(
            collective_id=0, has_side_effects=True, vmem_limit_bytes=limit
        ),
    )(modes, directions, locked, perm_class, perm_table, locked_count)
    new_modes, new_dirs, ritz, corr = pl.pallas_call(
        finish,
        out_shape=(
            jax.ShapeDtypeStruct(modes.shape, F32),
            jax.ShapeDtypeStruct(modes.shape, F32),
            jax.ShapeDtypeStruct((ACTIVE,), F32),
            jax.ShapeDtypeStruct(corr.shape, F32),
        ),
        in_specs=[hbm, hbm, hbm],
        out_specs=(hbm, hbm, smem, hbm),
        scratch_shapes=[
            pltpu.VMEM(sums.shape, F32),
            pltpu.VMEM(trial.shape, F32),
            pltpu.VMEM(corr.shape, F32),
            pltpu.VMEM(modes.shape, F32),
            pltpu.VMEM(modes.shape, F32),
            dma((6,)),
        ],
        compiler_params=pltpu.CompilerParams(vmem_limit_bytes=limit),
    )(sums, trial, corr)
    return new_modes, new_dirs, ritz, corr.T


def solution(mesh):
    placed = (
        P(None, "gx", "gy"),
        P(None, "gx", "gy"),
        P(None, "gx", "gy"),
        P("gx", "gy"),
        P(),
        P(),
    )
    return jax.shard_map(
        functools.partial(on_device, mesh.shape["gx"], mesh.shape["gy"]),
        mesh=mesh,
        in_specs=placed,
        out_specs=(P(None, "gx", "gy"), P(None, "gx", "gy"), P(), P()),
        check_vma=False,
    )
```

```python
import functools

import jax
import jax.numpy as jnp
from jax import lax
from jax.experimental import pallas as pl
from jax.experimental.pallas import tpu as pltpu
from jax.sharding import PartitionSpec as P

NZ = 64
ACTIVE = 4
SWEEPS = 3
RITZ = 3
OMEGA = 0.6
EPSILON = 1e-06
PRECISE = lax.Precision.HIGHEST
F32 = jnp.float32
REACH = SWEEPS


def iota(shape, dim):
    return lax.broadcasted_iota(jnp.int32, shape, dim)


def nt(a, b):
    return lax.dot_general(a, b, (((1,), (1,)), ((), ())), precision=PRECISE, preferred_element_type=F32)


def nn(a, b):
    return lax.dot_general(a, b, (((1,), (0,)), ((), ())), precision=PRECISE, preferred_element_type=F32)


def lanes(u, by):
    return pltpu.roll(u, by % 128, u.ndim - 1)


def subs(u, by):
    return pltpu.roll(u, by % 8, u.ndim - 2)


def face_value(a, b):
    both = (a > 0) & (b > 0)
    return jnp.where(both, 2.0 * a * b / jnp.where(both, a + b, 1.0), 2.0 * (a + b))


BF16 = jnp.bfloat16


def split(a):
    high = a.astype(BF16)
    return high, (a - high.astype(F32)).astype(BF16)


def dot_split(a, b_high, b_low, dims):
    rows = a.shape[0]
    high = a.astype(BF16).astype(F32)
    stack = jnp.concatenate([high, a - high], axis=0).astype(BF16)
    dims = (dims, ((), ()))
    one = lax.dot_general(stack, b_high, dims, preferred_element_type=F32)
    two = lax.dot_general(high.astype(BF16), b_low, dims, preferred_element_type=F32)
    return one[:rows] + (one[rows:] + two)


NT = ((1,), (1,))
NN = ((1,), (0,))


class Marks:
    def __init__(self):
        lane = iota((8, 128), 1)
        sub = iota((8, 128), 0)
        self.lane = lane
        self.sub = sub
        self.z = lane % NZ
        self.half0 = lane < 64
        self.par0 = sub < 4
        self.even = lane % 2 == 0
        self.quad = lane % 4 < 2


def neighbours(m, u):
    inner = u[1:-1, 1:-1]
    zl = jnp.where(m.z == 0, 0.0, lanes(inner, 1))
    zu = jnp.where(m.z == NZ - 1, 0.0, lanes(inner, -1))
    flip = lanes(u[1:-1], 64)
    yl = jnp.where(m.half0, flip[:, :-2], flip[:, 1:-1])
    yu = jnp.where(m.half0, flip[:, 1:-1], flip[:, 2:])
    turn = subs(u[:, 1:-1], 4)
    xl = jnp.where(m.par0, turn[:-2], turn[1:-1])
    xu = jnp.where(m.par0, turn[1:-1], turn[2:])
    return xl, xu, yl, yu, zl, zu


def total(parts):
    out = parts[0]
    for part in parts[1:]:
        out = out + part
    return out


def fine_coef(m, k):
    inner = k[1:-1, 1:-1]
    faces = [face_value(near, inner) for near in neighbours(m, k)]
    return [total(faces)] + faces


def stencil(m, u, coef):
    near = neighbours(m, u)
    return coef[0] * u[1:-1, 1:-1] - total([c * v for c, v in zip(coef[1:], near)])


def inverse(diag, inside):
    return jnp.where(inside, OMEGA / jnp.where(inside, diag, 1.0), 0.0)


def pair_x(u):
    return u + subs(u, 4)


def pair_y(u):
    return u + lanes(u, 64)


def pair_z(m, u):
    return u + jnp.where(m.even, lanes(u, -1), lanes(u, 1))


def pair_z2(m, u):
    return u + jnp.where(m.quad, lanes(u, -2), lanes(u, 2))


def middle_coef(m, c):
    xl = pair_z(m, pair_y(jnp.where(m.par0, c[1], subs(c[1], 4))))
    xu = pair_z(m, pair_y(jnp.where(m.par0, subs(c[2], 4), c[2])))
    yl = pair_z(m, pair_x(jnp.where(m.half0, c[3], lanes(c[3], 64))))
    yu = pair_z(m, pair_x(jnp.where(m.half0, lanes(c[4], 64), c[4])))
    zl = pair_y(pair_x(jnp.where(m.even, c[5], lanes(c[5], 1))))
    zu = pair_y(pair_x(jnp.where(m.even, lanes(c[6], -1), c[6])))
    faces = [xl, xu, yl, yu, zl, zu]
    return [total(faces)] + faces


def middle_stencil(m, u, coef):
    inner = u[1:-1, 1:-1]
    zl = jnp.where(m.z < 2, 0.0, lanes(inner, 2))
    zu = jnp.where(m.z >= NZ - 2, 0.0, lanes(inner, -2))
    near = [u[:-2, 1:-1], u[2:, 1:-1], u[1:-1, :-2], u[1:-1, 2:], zl, zu]
    return coef[0] * inner - total([c * v for c, v in zip(coef[1:], near)])


def coarse_pack(m, mid):
    _, xl, xu, yl, yu, zl, zu = mid
    out = jnp.zeros((8, 128), F32)
    for q in range(2):
        a, b = 2 * q, 2 * q + 1
        faces = [
            pair_z2(m, xl[0, a] + xl[0, b]),
            pair_z2(m, xu[1, a] + xu[1, b]),
            pair_z2(m, yl[0, a] + yl[1, a]),
            pair_z2(m, yu[0, b] + yu[1, b]),
        ]
        low = zl[0, a] + zl[0, b] + zl[1, a] + zl[1, b]
        high = zu[0, a] + zu[0, b] + zu[1, a] + zu[1, b]
        faces.append(jnp.where(m.quad, low, lanes(low, 2)))
        faces.append(jnp.where(m.quad, lanes(high, -2), high))
        for k in range(6):
            spot = (m.sub == 4 * q + k % 4) & (m.half0 if k < 4 else ~m.half0)
            out = jnp.where(spot, faces[k], out)
    return out


def flat(u):
    return jnp.concatenate([u[x, y] for x in range(2) for y in range(4)], axis=1)


def unflat(u):
    tiles = [u[:, 128 * i : 128 * (i + 1)] for i in range(8)]
    return jnp.stack([jnp.stack(tiles[:4]), jnp.stack(tiles[4:])])


def fold_locked(m, g):
    g = jnp.where(m.par0 == m.half0, g, 0.0)
    return pair_y(pair_x(g))


def spread_locked(m, c):
    return jnp.where(m.par0 == m.half0, c, 0.0)


def kernel(
    ngx,
    ngy,
    modes_hbm,
    dirs_hbm,
    locked_hbm,
    class_hbm,
    table_ref,
    count_ref,
    sums_ref,
    trial_ref,
    corr_ref,
    kh,
    xp,
    e0h,
    e1h,
    ccg,
    r2g,
    e2s,
    lxlow,
    lxhigh,
    lylow,
    lyhigh,
    lysend,
    al,
    lst,
    l_high,
    l_low,
    modes_ref,
    dirs_ref,
    locked_ref,
    class_ref,
    ins,
    by1,
    bx1,
    by2,
    bx2,
    by3,
    bx3,
    hs,
    hr,
    rs,
    rr,
    cs,
    cr,
):
    loads = [
        pltpu.make_async_copy(src, dst, ins.at[i])
        for i, (src, dst) in enumerate(
            [(class_hbm, class_ref), (modes_hbm, modes_ref), (dirs_hbm, dirs_ref), (locked_hbm, locked_ref)]
        )
    ]
    for load in loads:
        load.start()
    m = Marks()
    gx, gy = lax.axis_index("gx"), lax.axis_index("gy")
    count = ngx * ngy
    cells = float(4 * 512 * count)
    pending = []

    for buf in (kh, xp, e0h, e1h, ccg, r2g, e2s, lxlow, lxhigh, lylow, lyhigh):
        buf[...] = jnp.zeros(buf.shape, F32)

    barrier = pltpu.get_barrier_semaphore()

    def greet(tx, ty):
        pl.semaphore_signal(barrier, inc=1, device_id=(tx, ty), device_id_type=pl.DeviceIdType.MESH)

    for i in range(1, ngx):
        greet(lax.rem(gx + i, ngx), gy)
    for i in range(1, ngy):
        greet(gx, lax.rem(gy + i, ngy))
    for dx in (-1, 1):
        for dy in (-1, 1):
            pl.when(
                (gx + dx >= 0) & (gx + dx < ngx) & (gy + dy >= 0) & (gy + dy < ngy)
            )(functools.partial(greet, gx + dx, gy + dy))
    beside_x = jnp.where(gx > 0, 1, 0) + jnp.where(gx < ngx - 1, 1, 0)
    beside_y = jnp.where(gy > 0, 1, 0) + jnp.where(gy < ngy - 1, 1, 0)
    greeted = ngx + ngy - 2 + beside_x * beside_y

    def remote(src, dst, send, recv, tx, ty):
        return pltpu.make_async_remote_copy(
            src_ref=src, dst_ref=dst, send_sem=send, recv_sem=recv, device_id=(tx, ty),
            device_id_type=pl.DeviceIdType.MESH,
        )

    def inside(tx, ty):
        return (tx >= 0) & (tx < ngx) & (ty >= 0) & (ty < ngy)

    def halo(slot, view, w, corners):
        def span(d, n):
            if d > 0:
                return pl.ds(n, w), pl.ds(0, w)
            if d < 0:
                return pl.ds(w, w), pl.ds(w + n, w)
            return pl.ds(w, n), pl.ds(w, n)

        copies = []
        for dx in (-1, 0, 1):
            for dy in (-1, 0, 1):
                if (dx, dy) == (0, 0) or (dx and dy and not corners):
                    continue
                (sx, tx), (sy, ty) = span(dx, 2), span(dy, 4)
                n = (dx + 1) * 3 + dy + 1
                copy = remote(view(sx, sy), view(tx, ty), hs.at[slot, n], hr.at[slot, n], gx + dx, gy + dy)
                to, frm = inside(gx + dx, gy + dy), inside(gx - dx, gy - dy)
                pl.when(to)(copy.start)
                copies.append((copy, frm))
                pending.append((copy, to))

        def arrive():
            for copy, frm in copies:
                pl.when(frm)(copy.wait_recv)

        return arrive

    def share(slot, buf, mine, n, axis, view):
        copies = []
        for i in range(1, n):
            to, frm = lax.rem(mine + i, n), lax.rem(mine + n - i, n)
            where = (gx, to) if axis == "gy" else (to, gy)
            back = (gx, frm) if axis == "gy" else (frm, gy)
            copy = remote(view(buf, mine), view(buf, mine), rs.at[slot, i], rr.at[slot, i], *where)
            copy.start()
            pending.append((copy, None))
            copies.append(remote(view(buf, frm), view(buf, frm), rs.at[slot, i], rr.at[slot, i], *back))

        def arrive():
            for copy in copies:
                copy.wait_recv()

        return arrive

    def reduce_start(slot, val, bufy):
        bufy[gy] = val
        return share(slot, bufy, gy, ngy, "gy", lambda b, i: b.at[i])

    def reduce_next(slot, first, bufy, bufx):
        first()
        bufx[gx] = total([bufy[j] for j in range(ngy)])
        return share(slot + 1, bufx, gx, ngx, "gx", lambda b, i: b.at[i])

    def reduce_end(slot, first, bufy, bufx):
        reduce_next(slot, first, bufy, bufx)()
        return total([bufx[j] for j in range(ngx)])

    def gather_start(slot, buf, val):
        buf[REACH, gy] = val
        return share(slot, buf, gy, ngy, "gy", lambda b, i: b.at[REACH, i])

    def gather_next(slot, first, buf):
        first()
        copies = []
        for d in range(-REACH, REACH + 1):
            if d == 0:
                continue
            copy = remote(
                buf.at[REACH], buf.at[REACH - d], cs.at[slot, d + REACH], cr.at[slot, d + REACH], gx + d, gy
            )
            to, frm = inside(gx + d, gy), inside(gx - d, gy)
            pl.when(to)(copy.start)
            copies.append((copy, frm))
            pending.append((copy, to))

        def arrive():
            for copy, frm in copies:
                pl.when(frm)(copy.wait_recv)

        return arrive

    for load in loads[:3]:
        load.wait()
    classes = class_ref[...]
    conduct = jnp.zeros(classes.shape, F32)
    for c in range(table_ref.shape[0]):
        conduct = jnp.where(classes == c, table_ref[c], conduct)
    for x in range(4):
        for y in range(4):
            cut = slice(128 * y, 128 * (y + 1))
            rows = pl.ds(4 * (x % 2), 4)
            kh[2 + x // 2, 2 + y, rows, :] = jnp.broadcast_to(conduct[x : x + 1, cut], (4, 128))
            xp[0, 1 + x // 2, 1 + y, rows, :] = modes_ref[:, x, cut]
            xp[1, 1 + x // 2, 1 + y, rows, :] = dirs_ref[:, x, cut]
    pl.semaphore_wait(barrier, greeted)
    arrive_k = halo(0, lambda a, b: kh.at[a, b], 2, True)
    arrive_xp = halo(1, lambda a, b: xp.at[:, a, b], 1, False)

    loads[3].wait()
    nl = locked_ref.shape[0]
    for x in range(4):
        for y in range(4):
            cut = slice(128 * y, 128 * (y + 1))
            to = pl.ds(128 * ((x // 2) * 4 + y), 128)
            lst[pl.ds(64 * (x % 2), nl), to] = locked_ref[:, x, cut]
            lst[pl.ds(64 * (x % 2) + nl, 4), to] = modes_ref[:, x, cut]

    def tile(x, y, par):
        return lst[64 * par : 64 * par + 64, 128 * (4 * x + y) : 128 * (4 * x + y) + 128]

    def column(x, y):
        return lst[:, 128 * (4 * x + y) : 128 * (4 * x + y) + 128]

    wide_lane = iota((128, 128), 1) < 64
    lysend[0] = jnp.where(wide_lane, lanes(column(0, 3), 64), column(1, 3))
    lysend[1] = jnp.where(wide_lane, column(0, 0), lanes(column(1, 0), 64))
    locked_copies = []
    for n, (src, dst, dx, dy) in enumerate(
        [
            (lst.at[pl.ds(64, 64), pl.ds(512, 512)], lxlow, 1, 0),
            (lst.at[pl.ds(0, 64), pl.ds(0, 512)], lxhigh, -1, 0),
            (lysend.at[0], lylow, 0, 1),
            (lysend.at[1], lyhigh, 0, -1),
        ]
    ):
        copy = remote(src, dst, hs.at[4, n], hr.at[4, n], gx + dx, gy + dy)
        to, frm = inside(gx + dx, gy + dy), inside(gx - dx, gy - dy)
        pl.when(to)(copy.start)
        pending.append((copy, to))
        locked_copies.append((copy, frm))

    own_x = xp[0, 1:3, 1:5]
    own_p = xp[1, 1:3, 1:5]
    x8 = flat(own_x)
    high, low = split(lst[...])
    l_high[...] = high
    l_low[...] = low
    mode_dots = fold_locked(m, dot_split(x8, l_high[...], l_low[...], NT))

    arrive_k()
    arrive_xp()
    own_coef = fine_coef(m, kh[1:5, 1:7])
    image_x = stencil(m, xp[0], own_coef)
    image_x8 = flat(image_x)
    image_dots = fold_locked(m, dot_split(image_x8, l_high[...], l_low[...], NT))
    first = reduce_start(0, jnp.where(m.half0, image_dots, mode_dots), by1)

    wide = fine_coef(m, kh[...])
    in_grid = kh[1:5, 1:7] > 0
    dinv0 = inverse(wide[0], in_grid)
    second = reduce_next(0, first, by1, bx1)
    mid = middle_coef(m, wide)
    dinv1 = inverse(mid[0], in_grid)
    own_mid = [c[1:3, 1:5] for c in mid]
    first_c = gather_start(6, ccg, coarse_pack(m, own_mid))
    image_p = stencil(m, xp[1], own_coef)
    second()
    sums = total([bx1[j] for j in range(ngx)])

    f_of = m.sub % 4
    top = jnp.sum(jnp.where(m.lane == nl + f_of, sums, 0.0), axis=1, keepdims=True)
    norm = jnp.sum(jnp.where(m.lane == 64 + nl + f_of, sums, 0.0), axis=1, keepdims=True)
    rayleigh = top / cells / (norm / cells + EPSILON)
    swapped = lanes(sums, 64)
    image_sum = jnp.where(m.half0, sums, swapped)
    mode_sum = jnp.where(m.half0, swapped, sums)
    j_of = m.lane % 64
    in_use = (j_of < count_ref[0]) & (j_of < nl)
    coupling = jnp.where(in_use, (image_sum - mode_sum * rayleigh) / cells, 0.0)
    coupling = jnp.where(j_of == nl + f_of, rayleigh, coupling)
    residual = image_x - unflat(
        dot_split(spread_locked(m, coupling), l_high[...], l_low[...], NN)
    )

    e0h[2:4, 2:6] = residual * dinv0[1:3, 1:5]
    arrive_e0 = halo(2, lambda a, b: e0h.at[a, b], 2, True)
    arrive_c = gather_next(0, first_c, ccg)
    for copy, frm in locked_copies:
        pl.when(frm)(copy.wait_recv)
    low64 = iota((64, 128), 1) < 64
    z_row = iota((1, 128), 1) % NZ
    for x in range(2):
        for par in range(2):
            rows = slice(64 * par, 64 * par + 64)
            flips = [lanes(tile(x, y, par), 64) for y in range(4)]
            before = lylow[rows] if x == 0 else lanes(lylow[rows], 64)
            after = lyhigh[rows] if x == 1 else lanes(lyhigh[rows], 64)
            flips = [before] + flips + [after]
            for y in range(4):
                u = tile(x, y, par)
                cut = slice(128 * y, 128 * y + 128)
                if par:
                    xl = tile(x, y, 0)
                    xu = tile(1, y, 0) if x == 0 else lxhigh[:, cut]
                else:
                    xl = tile(0, y, 1) if x == 1 else lxlow[:, cut]
                    xu = tile(x, y, 1)
                yl = jnp.where(low64, flips[y], flips[y + 1])
                yu = jnp.where(low64, flips[y + 1], flips[y + 2])
                c = [k[x, y, 4 * par : 4 * par + 1] for k in own_coef]
                near = c[1] * xl + c[2] * xu + c[3] * yl + c[4] * yu
                near = near + jnp.where(z_row == 0, 0.0, c[5]) * lanes(u, 1)
                near = near + jnp.where(z_row == NZ - 1, 0.0, c[6]) * lanes(u, -1)
                al[rows, 128 * (4 * x + y) : 128 * (4 * x + y) + 128] = c[0] * u - near

    arrive_e0()
    e0_wide = e0h[...]
    r1 = e0_wide[1:5, 1:7] * (wide[0] * (1.0 / OMEGA)) - stencil(m, e0_wide, wide)
    r1 = pair_z(m, pair_y(pair_x(r1)))
    e1_near = r1 * dinv1
    e1h[2:4, 2:6] = e1_near[1:3, 1:5]
    arrive_e1 = halo(3, lambda a, b: e1h.at[a, b], 2, True)
    r2 = r1[1:3, 1:5] - middle_stencil(m, e1_near, own_mid)
    r2 = r2[0] + r2[1]
    r2 = jnp.where(m.par0, r2[0] + r2[1], r2[2] + r2[3])
    first_r = gather_start(7, r2g, pair_z2(m, r2))
    arrive_c()
    lines = 2 * ngy
    shift = 4.0 / float(lines * lines)
    faces = []
    for y in range(lines):
        tile = ccg[:, y // 2]
        other = lanes(tile, 64)
        low, high = jnp.where(m.half0, tile, other), jnp.where(m.half0, other, tile)
        row = 4 * (y % 2)
        one = []
        for k in range(6):
            src = low if k < 4 else high
            one.append(jnp.broadcast_to(src[:, row + k % 4 : row + k % 4 + 1], (2 * REACH + 1, 4, 128)))
        faces.append(one)
    z4 = m.z[:4]
    pivots, uppers, diags, dinv2 = [], [], [], []
    for y in range(lines):
        xl, xu, yl, yu, zl, zu = faces[y]
        diag = xl + xu + yl + yu + zl + zu
        known = diag > 0
        main = yl + yu + shift * (xl + xu + zl + zu)
        if y:
            main = main - yl * uppers[y - 1]
        piv = 1.0 / jnp.where(known, main, 1.0)
        pivots.append(piv)
        uppers.append(yu * piv)
        diags.append(diag)
        dinv2.append(inverse(diag, known))
        faces[y][4] = jnp.where(z4 < 4, 0.0, zl)
        faces[y][5] = jnp.where(z4 >= NZ - 4, 0.0, zu)

    arrive_r = gather_next(1, first_r, r2g)
    square = []
    for left in (lst[...], al[...]):
        whole = dot_split(left, l_high[...], l_low[...], NT)
        square.append(whole[:64, :64] + whole[64:, 64:])
    first_s = reduce_start(4, jnp.concatenate(square, axis=1), by3)
    arrive_r()

    source = [r2g[:, y // 2, 4 * (y % 2) : 4 * (y % 2) + 4] for y in range(lines)]
    held = []
    for y in range(lines):
        right = source[y] if y == 0 else source[y] + faces[y][2] * held[y - 1]
        held.append(right * pivots[y])
    for y in range(lines - 2, -1, -1):
        held[y] = held[y] + uppers[y] * held[y + 1]
    for sweep in range(1, SWEEPS):
        nxt = []
        for y in range(lines):
            cut = slice(sweep, 2 * REACH + 1 - sweep)
            c = [f[cut] for f in faces[y]]
            u = held[y]
            mid_u = u[1:-1]
            beside = c[0] * u[:-2] + c[1] * u[2:]
            if y:
                beside = beside + c[2] * held[y - 1][1:-1]
            if y < lines - 1:
                beside = beside + c[3] * held[y + 1][1:-1]
            beside = beside + c[4] * lanes(mid_u, 4) + c[5] * lanes(mid_u, -4)
            off = source[y][cut] - (diags[y][cut] * mid_u - beside)
            nxt.append(mid_u + dinv2[y][cut] * off)
        held = nxt
    for y in range(lines):
        e2s[1 + y] = held[y]
    near = e2s[pl.ds(2 * gy, 4)]
    near = jnp.concatenate([near, near], axis=2)

    arrive_e1()
    e1_wide = e1h[...]
    e1_wide = jnp.stack(
        [jnp.stack([e1_wide[a, b] + near[b // 2, a // 2] for b in range(8)]) for a in range(6)]
    )
    e1 = e1_wide[1:5, 1:7] + e1h[1:5, 1:7] - dinv1 * middle_stencil(m, e1_wide, mid)
    e0 = e0_wide[1:5, 1:7] + e1
    edge_y, edge_x = jnp.zeros((4, 1, 8, 128), F32), jnp.zeros((1, 8, 8, 128), F32)
    e0_rim = jnp.concatenate([edge_y, e0, edge_y], axis=1)
    e0_rim = jnp.concatenate([edge_x, e0_rim, edge_x], axis=0)
    precond_wide = e0 + e0_wide[1:5, 1:7] - dinv0 * stencil(m, e0_rim, wide)
    precond = precond_wide[1:3, 1:5]
    image_w = stencil(m, precond_wide, own_coef)
    precond8 = flat(precond)
    fields = jnp.concatenate([precond8, flat(own_p), flat(image_w), flat(image_p)], axis=0)
    with_locked = dot_split(fields, l_high[...], l_low[...], NT)
    f_pc, f_p, f_apc, f_ap = [fold_locked(m, with_locked[8 * i : 8 * i + 8]) for i in range(4)]
    cross = jnp.where(m.par0, jnp.where(m.half0, f_pc, f_apc), jnp.where(m.half0, f_p, f_ap))
    f_high, f_low = split(fields[:16])
    among = dot_split(fields, f_high, f_low, NT)
    row, col = iota((32, 16), 0), iota((32, 16), 1)
    among = jnp.where((row // 4) % 2 == (col // 4) % 2, among, 0.0)
    among = jnp.concatenate(
        [among[:16], jnp.zeros((16, 48), F32), among[16:], jnp.zeros((16, 48), F32)], axis=1
    )
    among = [among[:8], among[8:]]
    among = [u + subs(u, 4) for u in among]
    own = jnp.where(m.par0, among[0], among[1])
    own = own + lanes(own, -4)
    first = reduce_start(2, jnp.concatenate([cross, own], axis=0), by2)
    second_s = reduce_next(4, first_s, by3, bx3)
    late = reduce_end(2, first, by2, bx2) / cells
    cross, own = late[:8], late[8:]
    corr = jnp.where(in_use & m.half0 & m.par0, cross, 0.0)
    corr_ref[...] = corr[:ACTIVE, : corr_ref.shape[1]]
    twice = corr + subs(corr, 4)
    twice = twice + lanes(twice, 64)
    projected8 = precond8 - dot_split(spread_locked(m, twice), l_high[...], l_low[...], NN)
    trial_ref[...] = jnp.concatenate([x8, projected8, flat(own_p)], axis=0)
    second_s()
    inner = total([bx3[j] for j in range(ngx)]) / cells

    zero = jnp.zeros((8, 64), F32)
    low8 = iota((8, 64), 0) < 4
    spot = iota((8, 64), 1) == nl + iota((8, 64), 0)
    combine = jnp.concatenate([jnp.where(low8 & spot, 1.0, 0.0), -corr[:, :64], zero], axis=0)
    grams = []
    for i in range(2):
        cut = slice(64 * i, 64 * i + 64)
        part = cross[:, cut]
        direct = jnp.concatenate(
            [zero, jnp.where(low8, part, 0.0), jnp.where(low8, subs(part, 4), 0.0)], axis=0
        )
        gram = nt(nn(combine, inner[:, cut]) + direct, combine) + nt(combine, direct)
        some = own[:, 64 * i : 64 * i + 16]
        some = jnp.where((iota((8, 16), 1) // 4) % 2 == 0, some, 0.0)
        low16 = iota((8, 16), 0) < 4
        some = jnp.concatenate(
            [jnp.zeros((8, 16), F32), jnp.where(low16, some, 0.0), jnp.where(low16, subs(some, 4), 0.0)], axis=0
        )
        grams.append(gram + jnp.concatenate([jnp.zeros((24, 8), F32), some], axis=1))
    sums_ref[...] = jnp.concatenate(
        [grams[0], jnp.zeros((24, 8), F32), grams[1], jnp.zeros((24, 72), F32)], axis=1
    )

    for copy, to in pending:
        if to is None:
            copy.wait_send()
        else:
            pl.when(to)(copy.wait_send)


def finish(
    sums_hbm, trial_hbm, corr_hbm, new_modes_hbm, new_dirs_hbm, ritz_ref, corr_out,
    sums_ref, trial_ref, corr_ref, new_modes_ref, new_dirs_ref, sems,
):
    loads = [
        pltpu.make_async_copy(sums_hbm, sums_ref, sems.at[0]),
        pltpu.make_async_copy(trial_hbm, trial_ref, sems.at[1]),
        pltpu.make_async_copy(corr_hbm, corr_ref, sems.at[2]),
    ]
    for load in loads:
        load.start()
    m = Marks()
    row, col = iota((24, 128), 0), iota((24, 128), 1)
    for load in loads:
        load.wait()
    store_corr = pltpu.make_async_copy(corr_ref, corr_out, sems.at[3])
    store_corr.start()
    sums = sums_ref[...]
    real = row % 8 < 4
    table = jnp.where(real & (col < 64) & (col % 8 < 4), sums, 0.0)
    table = jnp.where(real & (col == row + 64), 1.0, table)
    pivots_at = [8 * g + f for g in range(3) for f in range(4)]

    def eliminate(work, order, rows):
        for k in order:
            pivot = work[k : k + 1, k : k + 1]
            scale = lax.rsqrt(pivot)
            line = work[k : k + 1, :] * scale
            factor = jnp.where(rows > k, work[:, k : k + 1] * scale, 0.0)
            work = jnp.where(rows == k, line, work - factor * line)
        return work

    work = eliminate(table, pivots_at, row)
    half = jnp.where(col < 24, lanes(work, -32), 0.0)
    linv = jnp.where(col < 24, lanes(work, -64), 0.0)
    reduced = 0.5 * (nt(half, linv) + nt(linv, half))
    reduced = jnp.concatenate([reduced, jnp.zeros((24, 104), F32)], axis=1)
    spectral = jnp.sum(jnp.where(row == col, reduced, 0.0), keepdims=True)
    raised = jnp.where((row == col) & real, spectral, 0.0) - reduced
    full = jnp.concatenate([raised, jnp.zeros((104, 128), F32)], axis=0)
    reduced_full = jnp.concatenate([reduced, jnp.zeros((104, 128), F32)], axis=0)
    basis = jnp.where(m.par0, raised[:8], 0.0)
    for step in range(RITZ - 1):
        basis = nn(basis, full)
    square = nt(basis, basis)
    small = jnp.concatenate([square, jnp.zeros((8, 120), F32)], axis=1) + lanes(basis, 32)
    small = eliminate(small, range(4), m.sub)
    basis = jnp.where((m.lane < 24) & m.par0, lanes(small, -32), 0.0)
    ritz = jnp.sum(basis * nn(basis, reduced_full), axis=1, keepdims=True)
    for k in range(ACTIVE):
        ritz_ref[k] = ritz[k, 0]
    linv_full = jnp.concatenate([linv, jnp.zeros((104, 128), F32)], axis=0)
    coef = nn(basis, linv_full)
    coef = coef + lanes(coef, 4)
    coef = coef + subs(coef, 4)
    coef = jnp.where(m.par0 == ((m.lane // 4) % 2 == 0), coef, 0.0)[:, :24]
    f_high, f_low = split(trial_ref[...])
    later = jnp.where(iota((8, 24), 1) >= 8, coef, 0.0)
    mixed = dot_split(jnp.concatenate([coef, later], axis=0), f_high, f_low, NN)
    modes8, dirs8 = mixed[:8], mixed[8:]
    for x in range(4):
        for y in range(4):
            cut = slice(128 * y, 128 * (y + 1))
            frm = slice(128 * ((x // 2) * 4 + y), 128 * ((x // 2) * 4 + y + 1))
            rows = slice(4 * (x % 2), 4 * (x % 2) + 4)
            new_modes_ref[:, x, cut] = modes8[rows, frm]
            new_dirs_ref[:, x, cut] = dirs8[rows, frm]
    stores = [
        pltpu.make_async_copy(new_modes_ref, new_modes_hbm, sems.at[4]),
        pltpu.make_async_copy(new_dirs_ref, new_dirs_hbm, sems.at[5]),
    ]
    for store in stores:
        store.start()
    for store in stores + [store_corr]:
        store.wait()


def on_device(ngx, ngy, modes, directions, locked, perm_class, perm_table, locked_count):
    vmem = pl.BlockSpec(memory_space=pltpu.VMEM)
    smem = pl.BlockSpec(memory_space=pltpu.SMEM)
    dma = pltpu.SemaphoreType.DMA
    wide = 2 * REACH + 1
    hbm = pl.BlockSpec(memory_space=pltpu.HBM)
    limit = 64 * 1024 * 1024 - 65536
    sums, trial, corr = pl.pallas_call(
        functools.partial(kernel, ngx, ngy),
        out_shape=(
            jax.ShapeDtypeStruct((24, 128), F32),
            jax.ShapeDtypeStruct((24, 1024), F32),
            jax.ShapeDtypeStruct((ACTIVE, locked.shape[0]), F32),
        ),
        in_specs=[hbm, hbm, hbm, hbm, smem, smem],
        out_specs=(vmem, vmem, vmem),
        scratch_shapes=[
            pltpu.VMEM((6, 8, 8, 128), F32),
            pltpu.VMEM((2, 4, 6, 8, 128), F32),
            pltpu.VMEM((6, 8, 8, 128), F32),
            pltpu.VMEM((6, 8, 8, 128), F32),
            pltpu.VMEM((wide, ngy, 8, 128), F32),
            pltpu.VMEM((wide, ngy, 8, 128), F32),
            pltpu.VMEM((2 * ngy + 2, 3, 4, 128), F32),
            pltpu.VMEM((64, 512), F32),
            pltpu.VMEM((64, 512), F32),
            pltpu.VMEM((128, 128), F32),
            pltpu.VMEM((128, 128), F32),
            pltpu.VMEM((2, 128, 128), F32),
            pltpu.VMEM((128, 1024), F32),
            pltpu.VMEM((128, 1024), F32),
            pltpu.VMEM((128, 1024), BF16),
            pltpu.VMEM((128, 1024), BF16),
            pltpu.VMEM(modes.shape, F32),
            pltpu.VMEM(directions.shape, F32),
            pltpu.VMEM(locked.shape, F32),
            pltpu.VMEM(perm_class.shape, jnp.int32),
            dma((4,)),
            pltpu.VMEM((ngy, 8, 128), F32),
            pltpu.VMEM((ngx, 8, 128), F32),
            pltpu.VMEM((ngy, 16, 128), F32),
            pltpu.VMEM((ngx, 16, 128), F32),
            pltpu.VMEM((ngy, 64, 128), F32),
            pltpu.VMEM((ngx, 64, 128), F32),
            dma((5, 9)),
            dma((5, 9)),
            dma((8, max(ngx, ngy))),
            dma((8, max(ngx, ngy))),
            dma((2, wide)),
            dma((2, wide)),
        ],
        compiler_params=pltpu.CompilerParams(
            collective_id=0, has_side_effects=True, vmem_limit_bytes=limit
        ),
    )(modes, directions, locked, perm_class, perm_table, locked_count)
    new_modes, new_dirs, ritz, corr = pl.pallas_call(
        finish,
        out_shape=(
            jax.ShapeDtypeStruct(modes.shape, F32),
            jax.ShapeDtypeStruct(modes.shape, F32),
            jax.ShapeDtypeStruct((ACTIVE,), F32),
            jax.ShapeDtypeStruct(corr.shape, F32),
        ),
        in_specs=[hbm, hbm, hbm],
        out_specs=(hbm, hbm, smem, hbm),
        scratch_shapes=[
            pltpu.VMEM(sums.shape, F32),
            pltpu.VMEM(trial.shape, F32),
            pltpu.VMEM(corr.shape, F32),
            pltpu.VMEM(modes.shape, F32),
            pltpu.VMEM(modes.shape, F32),
            dma((6,)),
        ],
        compiler_params=pltpu.CompilerParams(vmem_limit_bytes=limit),
    )(sums, trial, corr)
    return new_modes, new_dirs, ritz, corr.T


def solution(mesh):
    placed = (
        P(None, "gx", "gy"),
        P(None, "gx", "gy"),
        P(None, "gx", "gy"),
        P("gx", "gy"),
        P(),
        P(),
    )
    return jax.shard_map(
        functools.partial(on_device, mesh.shape["gx"], mesh.shape["gy"]),
        mesh=mesh,
        in_specs=placed,
        out_specs=(P(None, "gx", "gy"), P(None, "gx", "gy"), P(), P()),
        check_vma=False,
    )
```

```python
import functools

import jax
import jax.numpy as jnp
from jax import lax
from jax.experimental import pallas as pl
from jax.experimental.pallas import tpu as pltpu
from jax.sharding import PartitionSpec as P

NZ = 64
ACTIVE = 4
SWEEPS = 3
RITZ = 3
OMEGA = 0.6
EPSILON = 1e-06
PRECISE = lax.Precision.HIGHEST
F32 = jnp.float32
REACH = SWEEPS


def iota(shape, dim):
    return lax.broadcasted_iota(jnp.int32, shape, dim)


def nt(a, b):
    return lax.dot_general(a, b, (((1,), (1,)), ((), ())), precision=PRECISE, preferred_element_type=F32)


def nn(a, b):
    return lax.dot_general(a, b, (((1,), (0,)), ((), ())), precision=PRECISE, preferred_element_type=F32)


def lanes(u, by):
    return pltpu.roll(u, by % 128, u.ndim - 1)


def subs(u, by):
    return pltpu.roll(u, by % 8, u.ndim - 2)


def face_value(a, b):
    both = (a > 0) & (b > 0)
    return jnp.where(both, 2.0 * a * b / jnp.where(both, a + b, 1.0), 2.0 * (a + b))


BF16 = jnp.bfloat16


def split(a):
    high = a.astype(BF16)
    return high, (a - high.astype(F32)).astype(BF16)


def dot_split(a, b_high, b_low, dims):
    rows = a.shape[0]
    high = a.astype(BF16).astype(F32)
    stack = jnp.concatenate([high, a - high], axis=0).astype(BF16)
    dims = (dims, ((), ()))
    one = lax.dot_general(stack, b_high, dims, preferred_element_type=F32)
    two = lax.dot_general(high.astype(BF16), b_low, dims, preferred_element_type=F32)
    return one[:rows] + (one[rows:] + two)


NT = ((1,), (1,))
NN = ((1,), (0,))


class Marks:
    def __init__(self):
        lane = iota((8, 128), 1)
        sub = iota((8, 128), 0)
        self.lane = lane
        self.sub = sub
        self.z = lane % NZ
        self.half0 = lane < 64
        self.par0 = sub < 4
        self.even = lane % 2 == 0
        self.quad = lane % 4 < 2


def neighbours(m, u):
    inner = u[1:-1, 1:-1]
    zl = jnp.where(m.z == 0, 0.0, lanes(inner, 1))
    zu = jnp.where(m.z == NZ - 1, 0.0, lanes(inner, -1))
    flip = lanes(u[1:-1], 64)
    yl = jnp.where(m.half0, flip[:, :-2], flip[:, 1:-1])
    yu = jnp.where(m.half0, flip[:, 1:-1], flip[:, 2:])
    turn = subs(u[:, 1:-1], 4)
    xl = jnp.where(m.par0, turn[:-2], turn[1:-1])
    xu = jnp.where(m.par0, turn[1:-1], turn[2:])
    return xl, xu, yl, yu, zl, zu


def total(parts):
    out = parts[0]
    for part in parts[1:]:
        out = out + part
    return out


def fine_coef(m, k):
    inner = k[1:-1, 1:-1]
    faces = [face_value(near, inner) for near in neighbours(m, k)]
    return [total(faces)] + faces


def stencil(m, u, coef):
    near = neighbours(m, u)
    return coef[0] * u[1:-1, 1:-1] - total([c * v for c, v in zip(coef[1:], near)])


def inverse(diag, inside):
    return jnp.where(inside, OMEGA / jnp.where(inside, diag, 1.0), 0.0)


def pair_x(u):
    return u + subs(u, 4)


def pair_y(u):
    return u + lanes(u, 64)


def pair_z(m, u):
    return u + jnp.where(m.even, lanes(u, -1), lanes(u, 1))


def pair_z2(m, u):
    return u + jnp.where(m.quad, lanes(u, -2), lanes(u, 2))


def middle_coef(m, c):
    xl = pair_z(m, pair_y(jnp.where(m.par0, c[1], subs(c[1], 4))))
    xu = pair_z(m, pair_y(jnp.where(m.par0, subs(c[2], 4), c[2])))
    yl = pair_z(m, pair_x(jnp.where(m.half0, c[3], lanes(c[3], 64))))
    yu = pair_z(m, pair_x(jnp.where(m.half0, lanes(c[4], 64), c[4])))
    zl = pair_y(pair_x(jnp.where(m.even, c[5], lanes(c[5], 1))))
    zu = pair_y(pair_x(jnp.where(m.even, lanes(c[6], -1), c[6])))
    faces = [xl, xu, yl, yu, zl, zu]
    return [total(faces)] + faces


def middle_stencil(m, u, coef):
    inner = u[1:-1, 1:-1]
    zl = jnp.where(m.z < 2, 0.0, lanes(inner, 2))
    zu = jnp.where(m.z >= NZ - 2, 0.0, lanes(inner, -2))
    near = [u[:-2, 1:-1], u[2:, 1:-1], u[1:-1, :-2], u[1:-1, 2:], zl, zu]
    return coef[0] * inner - total([c * v for c, v in zip(coef[1:], near)])


def coarse_pack(m, mid):
    _, xl, xu, yl, yu, zl, zu = mid
    out = jnp.zeros((8, 128), F32)
    for q in range(2):
        a, b = 2 * q, 2 * q + 1
        faces = [
            pair_z2(m, xl[0, a] + xl[0, b]),
            pair_z2(m, xu[1, a] + xu[1, b]),
            pair_z2(m, yl[0, a] + yl[1, a]),
            pair_z2(m, yu[0, b] + yu[1, b]),
        ]
        low = zl[0, a] + zl[0, b] + zl[1, a] + zl[1, b]
        high = zu[0, a] + zu[0, b] + zu[1, a] + zu[1, b]
        faces.append(jnp.where(m.quad, low, lanes(low, 2)))
        faces.append(jnp.where(m.quad, lanes(high, -2), high))
        for k in range(6):
            spot = (m.sub == 4 * q + k % 4) & (m.half0 if k < 4 else ~m.half0)
            out = jnp.where(spot, faces[k], out)
    return out


def flat(u):
    return jnp.concatenate([u[x, y] for x in range(2) for y in range(4)], axis=1)


def unflat(u):
    tiles = [u[:, 128 * i : 128 * (i + 1)] for i in range(8)]
    return jnp.stack([jnp.stack(tiles[:4]), jnp.stack(tiles[4:])])


def fold_locked(m, g):
    g = jnp.where(m.par0 == m.half0, g, 0.0)
    return pair_y(pair_x(g))


def spread_locked(m, c):
    return jnp.where(m.par0 == m.half0, c, 0.0)


def kernel(
    ngx,
    ngy,
    modes_hbm,
    dirs_hbm,
    locked_hbm,
    class_hbm,
    table_ref,
    count_ref,
    sums_ref,
    trial_ref,
    corr_ref,
    kh,
    xp,
    e0h,
    e1h,
    ccg,
    r2g,
    e2s,
    lxlow,
    lxhigh,
    lylow,
    lyhigh,
    lysend,
    al,
    lst,
    l_high,
    l_low,
    modes_ref,
    dirs_ref,
    locked_ref,
    class_ref,
    ins,
    by1,
    by2,
    bx2,
    by3,
    bx3,
    hs,
    hr,
    rs,
    rr,
    cs,
    cr,
    os,
    orr,
    gs,
    gr,
):
    loads = [
        pltpu.make_async_copy(src, dst, ins.at[i])
        for i, (src, dst) in enumerate(
            [(class_hbm, class_ref), (modes_hbm, modes_ref), (dirs_hbm, dirs_ref), (locked_hbm, locked_ref)]
        )
    ]
    for load in loads:
        load.start()
    m = Marks()
    gx, gy = lax.axis_index("gx"), lax.axis_index("gy")
    count = ngx * ngy
    cells = float(4 * 512 * count)
    pending = []

    for buf in (kh, xp, e0h, e1h, ccg, r2g, e2s, lxlow, lxhigh, lylow, lyhigh):
        buf[...] = jnp.zeros(buf.shape, F32)

    barrier = pltpu.get_barrier_semaphore()

    def greet(tx, ty):
        pl.semaphore_signal(barrier, inc=1, device_id=(tx, ty), device_id_type=pl.DeviceIdType.MESH)

    def everyone(visit):
        if count <= 64:
            for i in range(1, count):
                visit(i, lax.rem(gx + i // ngy, ngx), lax.rem(gy + i % ngy, ngy))
        else:

            def body(i, carry):
                visit(i, lax.rem(gx + i // ngy, ngx), lax.rem(gy + lax.rem(i, ngy), ngy))
                return carry

            lax.fori_loop(1, count, body, 0)

    everyone(lambda i, tx, ty: greet(tx, ty))

    def remote(src, dst, send, recv, tx, ty):
        return pltpu.make_async_remote_copy(
            src_ref=src, dst_ref=dst, send_sem=send, recv_sem=recv, device_id=(tx, ty),
            device_id_type=pl.DeviceIdType.MESH,
        )

    def inside(tx, ty):
        return (tx >= 0) & (tx < ngx) & (ty >= 0) & (ty < ngy)

    def halo(slot, view, w, corners):
        def span(d, n):
            if d > 0:
                return pl.ds(n, w), pl.ds(0, w)
            if d < 0:
                return pl.ds(w, w), pl.ds(w + n, w)
            return pl.ds(w, n), pl.ds(w, n)

        copies = []
        for dx in (-1, 0, 1):
            for dy in (-1, 0, 1):
                if (dx, dy) == (0, 0) or (dx and dy and not corners):
                    continue
                (sx, tx), (sy, ty) = span(dx, 2), span(dy, 4)
                n = (dx + 1) * 3 + dy + 1
                copy = remote(view(sx, sy), view(tx, ty), hs.at[slot, n], hr.at[slot, n], gx + dx, gy + dy)
                to, frm = inside(gx + dx, gy + dy), inside(gx - dx, gy - dy)
                pl.when(to)(copy.start)
                copies.append((copy, frm))
                pending.append((copy, to))

        def arrive():
            for copy, frm in copies:
                pl.when(frm)(copy.wait_recv)

        return arrive

    def share(slot, buf, mine, n, axis, view):
        copies = []
        for i in range(1, n):
            to, frm = lax.rem(mine + i, n), lax.rem(mine + n - i, n)
            where = (gx, to) if axis == "gy" else (to, gy)
            back = (gx, frm) if axis == "gy" else (frm, gy)
            copy = remote(view(buf, mine), view(buf, mine), rs.at[slot, i], rr.at[slot, i], *where)
            copy.start()
            pending.append((copy, None))
            copies.append(remote(view(buf, frm), view(buf, frm), rs.at[slot, i], rr.at[slot, i], *back))

        def arrive():
            for copy in copies:
                copy.wait_recv()

        return arrive

    def spread_out(i, tx, ty):
        return remote(by1.at[gx, gy], by1.at[gx, gy], os.at[i], orr.at[i], tx, ty)

    def spread_in(i, tx, ty):
        fx = lax.rem(gx + ngx - i // ngy, ngx)
        fy = lax.rem(gy + ngy - (i % ngy if isinstance(i, int) else lax.rem(i, ngy)), ngy)
        return remote(by1.at[fx, fy], by1.at[fx, fy], os.at[i], orr.at[i], fx, fy)

    def rows_of(d, j):
        ty = lax.rem(gy + j, ngy)
        return remote(
            r2g.at[REACH, gy], r2g.at[REACH - d, gy], gs.at[d + REACH, j], gr.at[d + REACH, j], gx + d, ty
        )

    def rows_in(d, j):
        fy = lax.rem(gy + ngy - j, ngy)
        return remote(
            r2g.at[REACH, fy], r2g.at[REACH - d, fy], gs.at[d + REACH, j], gr.at[d + REACH, j], gx - d, fy
        )

    def across(visit, sign):
        for d in range(-REACH, REACH + 1):
            def row(d=d):
                for j in range(ngy):
                    if (d, j) != (0, 0):
                        visit(d, j)

            if d == 0:
                row()
            else:
                pl.when((gx + sign * d >= 0) & (gx + sign * d < ngx))(row)

    def reduce_start(slot, val, bufy):
        bufy[gy] = val
        return share(slot, bufy, gy, ngy, "gy", lambda b, i: b.at[i])

    def reduce_next(slot, first, bufy, bufx):
        first()
        bufx[gx] = total([bufy[j] for j in range(ngy)])
        return share(slot + 1, bufx, gx, ngx, "gx", lambda b, i: b.at[i])

    def reduce_end(slot, first, bufy, bufx):
        reduce_next(slot, first, bufy, bufx)()
        return total([bufx[j] for j in range(ngx)])

    def gather_start(slot, buf, val):
        buf[REACH, gy] = val
        return share(slot, buf, gy, ngy, "gy", lambda b, i: b.at[REACH, i])

    def gather_next(slot, first, buf):
        first()
        copies = []
        for d in range(-REACH, REACH + 1):
            if d == 0:
                continue
            copy = remote(
                buf.at[REACH], buf.at[REACH - d], cs.at[slot, d + REACH], cr.at[slot, d + REACH], gx + d, gy
            )
            to, frm = inside(gx + d, gy), inside(gx - d, gy)
            pl.when(to)(copy.start)
            copies.append((copy, frm))
            pending.append((copy, to))

        def arrive():
            for copy, frm in copies:
                pl.when(frm)(copy.wait_recv)

        return arrive

    for load in loads[:3]:
        load.wait()
    classes = class_ref[...]
    conduct = jnp.zeros(classes.shape, F32)
    for c in range(table_ref.shape[0]):
        conduct = jnp.where(classes == c, table_ref[c], conduct)
    for x in range(4):
        for y in range(4):
            cut = slice(128 * y, 128 * (y + 1))
            rows = pl.ds(4 * (x % 2), 4)
            kh[2 + x // 2, 2 + y, rows, :] = jnp.broadcast_to(conduct[x : x + 1, cut], (4, 128))
            xp[0, 1 + x // 2, 1 + y, rows, :] = modes_ref[:, x, cut]
            xp[1, 1 + x // 2, 1 + y, rows, :] = dirs_ref[:, x, cut]
    pl.semaphore_wait(barrier, count - 1)
    arrive_k = halo(0, lambda a, b: kh.at[a, b], 2, True)
    arrive_xp = halo(1, lambda a, b: xp.at[:, a, b], 1, False)

    loads[3].wait()
    nl = locked_ref.shape[0]
    for x in range(4):
        for y in range(4):
            cut = slice(128 * y, 128 * (y + 1))
            to = pl.ds(128 * ((x // 2) * 4 + y), 128)
            lst[pl.ds(64 * (x % 2), nl), to] = locked_ref[:, x, cut]
            lst[pl.ds(64 * (x % 2) + nl, 4), to] = modes_ref[:, x, cut]

    def tile(x, y, par):
        return lst[64 * par : 64 * par + 64, 128 * (4 * x + y) : 128 * (4 * x + y) + 128]

    def column(x, y):
        return lst[:, 128 * (4 * x + y) : 128 * (4 * x + y) + 128]

    wide_lane = iota((128, 128), 1) < 64
    lysend[0] = jnp.where(wide_lane, lanes(column(0, 3), 64), column(1, 3))
    lysend[1] = jnp.where(wide_lane, column(0, 0), lanes(column(1, 0), 64))
    locked_copies = []
    for n, (src, dst, dx, dy) in enumerate(
        [
            (lst.at[pl.ds(64, 64), pl.ds(512, 512)], lxlow, 1, 0),
            (lst.at[pl.ds(0, 64), pl.ds(0, 512)], lxhigh, -1, 0),
            (lysend.at[0], lylow, 0, 1),
            (lysend.at[1], lyhigh, 0, -1),
        ]
    ):
        copy = remote(src, dst, hs.at[4, n], hr.at[4, n], gx + dx, gy + dy)
        to, frm = inside(gx + dx, gy + dy), inside(gx - dx, gy - dy)
        pl.when(to)(copy.start)
        pending.append((copy, to))
        locked_copies.append((copy, frm))

    own_x = xp[0, 1:3, 1:5]
    own_p = xp[1, 1:3, 1:5]
    x8 = flat(own_x)
    high, low = split(lst[...])
    l_high[...] = high
    l_low[...] = low
    mode_dots = fold_locked(m, dot_split(x8, l_high[...], l_low[...], NT))

    arrive_k()
    arrive_xp()
    own_coef = fine_coef(m, kh[1:5, 1:7])
    image_x = stencil(m, xp[0], own_coef)
    image_x8 = flat(image_x)
    image_dots = fold_locked(m, dot_split(image_x8, l_high[...], l_low[...], NT))
    by1[gx, gy] = jnp.where(m.half0, image_dots, mode_dots)[:4]
    everyone(lambda i, tx, ty: spread_out(i, tx, ty).start())

    wide = fine_coef(m, kh[...])
    in_grid = kh[1:5, 1:7] > 0
    dinv0 = inverse(wide[0], in_grid)
    mid = middle_coef(m, wide)
    dinv1 = inverse(mid[0], in_grid)
    own_mid = [c[1:3, 1:5] for c in mid]
    first_c = gather_start(6, ccg, coarse_pack(m, own_mid))
    image_p = stencil(m, xp[1], own_coef)
    everyone(lambda i, tx, ty: spread_in(i, tx, ty).wait_recv())
    sums = jnp.sum(by1[...].reshape(count, 4, 128), axis=0)
    sums = jnp.concatenate([sums, sums], axis=0)

    f_of = m.sub % 4
    top = jnp.sum(jnp.where(m.lane == nl + f_of, sums, 0.0), axis=1, keepdims=True)
    norm = jnp.sum(jnp.where(m.lane == 64 + nl + f_of, sums, 0.0), axis=1, keepdims=True)
    rayleigh = top / cells / (norm / cells + EPSILON)
    swapped = lanes(sums, 64)
    image_sum = jnp.where(m.half0, sums, swapped)
    mode_sum = jnp.where(m.half0, swapped, sums)
    j_of = m.lane % 64
    in_use = (j_of < count_ref[0]) & (j_of < nl)
    coupling = jnp.where(in_use, (image_sum - mode_sum * rayleigh) / cells, 0.0)
    coupling = jnp.where(j_of == nl + f_of, rayleigh, coupling)
    residual = image_x - unflat(
        dot_split(spread_locked(m, coupling), l_high[...], l_low[...], NN)
    )

    e0h[2:4, 2:6] = residual * dinv0[1:3, 1:5]
    arrive_e0 = halo(2, lambda a, b: e0h.at[a, b], 2, True)
    arrive_c = gather_next(0, first_c, ccg)
    for copy, frm in locked_copies:
        pl.when(frm)(copy.wait_recv)
    low64 = iota((64, 128), 1) < 64
    z_row = iota((1, 128), 1) % NZ
    for x in range(2):
        for par in range(2):
            rows = slice(64 * par, 64 * par + 64)
            flips = [lanes(tile(x, y, par), 64) for y in range(4)]
            before = lylow[rows] if x == 0 else lanes(lylow[rows], 64)
            after = lyhigh[rows] if x == 1 else lanes(lyhigh[rows], 64)
            flips = [before] + flips + [after]
            for y in range(4):
                u = tile(x, y, par)
                cut = slice(128 * y, 128 * y + 128)
                if par:
                    xl = tile(x, y, 0)
                    xu = tile(1, y, 0) if x == 0 else lxhigh[:, cut]
                else:
                    xl = tile(0, y, 1) if x == 1 else lxlow[:, cut]
                    xu = tile(x, y, 1)
                yl = jnp.where(low64, flips[y], flips[y + 1])
                yu = jnp.where(low64, flips[y + 1], flips[y + 2])
                c = [k[x, y, 4 * par : 4 * par + 1] for k in own_coef]
                near = c[1] * xl + c[2] * xu + c[3] * yl + c[4] * yu
                near = near + jnp.where(z_row == 0, 0.0, c[5]) * lanes(u, 1)
                near = near + jnp.where(z_row == NZ - 1, 0.0, c[6]) * lanes(u, -1)
                al[rows, 128 * (4 * x + y) : 128 * (4 * x + y) + 128] = c[0] * u - near

    arrive_e0()
    e0_wide = e0h[...]
    r1 = e0_wide[1:5, 1:7] * (wide[0] * (1.0 / OMEGA)) - stencil(m, e0_wide, wide)
    r1 = pair_z(m, pair_y(pair_x(r1)))
    e1_near = r1 * dinv1
    e1h[2:4, 2:6] = e1_near[1:3, 1:5]
    arrive_e1 = halo(3, lambda a, b: e1h.at[a, b], 2, True)
    r2 = r1[1:3, 1:5] - middle_stencil(m, e1_near, own_mid)
    r2 = r2[0] + r2[1]
    r2 = jnp.where(m.half0, r2[0] + r2[1], r2[2] + r2[3])
    r2g[REACH, gy] = pair_z2(m, r2)[:4]
    across(lambda d, j: rows_of(d, j).start(), 1)
    arrive_c()
    lines = 2 * ngy
    shift = 4.0 / float(lines * lines)
    faces = []
    for y in range(lines):
        tile = ccg[:, y // 2]
        other = lanes(tile, 64)
        low, high = jnp.where(m.half0, tile, other), jnp.where(m.half0, other, tile)
        row = 4 * (y % 2)
        one = []
        for k in range(6):
            src = low if k < 4 else high
            one.append(jnp.broadcast_to(src[:, row + k % 4 : row + k % 4 + 1], (2 * REACH + 1, 4, 128)))
        faces.append(one)
    z4 = m.z[:4]
    pivots, uppers, diags, dinv2 = [], [], [], []
    for y in range(lines):
        xl, xu, yl, yu, zl, zu = faces[y]
        diag = xl + xu + yl + yu + zl + zu
        known = diag > 0
        main = yl + yu + shift * (xl + xu + zl + zu)
        if y:
            main = main - yl * uppers[y - 1]
        piv = 1.0 / jnp.where(known, main, 1.0)
        pivots.append(piv)
        uppers.append(yu * piv)
        diags.append(diag)
        dinv2.append(inverse(diag, known))
        faces[y][4] = jnp.where(z4 < 4, 0.0, zl)
        faces[y][5] = jnp.where(z4 >= NZ - 4, 0.0, zu)

    square = []
    for left in (lst[...], al[...]):
        whole = dot_split(left, l_high[...], l_low[...], NT)
        square.append(whole[:64, :64] + whole[64:, 64:])
    first_s = reduce_start(4, jnp.concatenate(square, axis=1), by3)
    across(lambda d, j: rows_in(d, j).wait_recv(), -1)

    source = []
    for y in range(lines):
        tile_y = r2g[:, y // 2]
        other = lanes(tile_y, 64)
        source.append(jnp.where(m.half0[:4], *((tile_y, other) if y % 2 == 0 else (other, tile_y))))
    held = []
    for y in range(lines):
        right = source[y] if y == 0 else source[y] + faces[y][2] * held[y - 1]
        held.append(right * pivots[y])
    for y in range(lines - 2, -1, -1):
        held[y] = held[y] + uppers[y] * held[y + 1]
    for sweep in range(1, SWEEPS):
        nxt = []
        for y in range(lines):
            cut = slice(sweep, 2 * REACH + 1 - sweep)
            c = [f[cut] for f in faces[y]]
            u = held[y]
            mid_u = u[1:-1]
            beside = c[0] * u[:-2] + c[1] * u[2:]
            if y:
                beside = beside + c[2] * held[y - 1][1:-1]
            if y < lines - 1:
                beside = beside + c[3] * held[y + 1][1:-1]
            beside = beside + c[4] * lanes(mid_u, 4) + c[5] * lanes(mid_u, -4)
            off = source[y][cut] - (diags[y][cut] * mid_u - beside)
            nxt.append(mid_u + dinv2[y][cut] * off)
        held = nxt
    for y in range(lines):
        e2s[1 + y] = held[y]
    near = e2s[pl.ds(2 * gy, 4)]
    near = jnp.concatenate([near, near], axis=2)

    arrive_e1()
    e1_wide = e1h[...]
    e1_wide = jnp.stack(
        [jnp.stack([e1_wide[a, b] + near[b // 2, a // 2] for b in range(8)]) for a in range(6)]
    )
    e1 = e1_wide[1:5, 1:7] + e1h[1:5, 1:7] - dinv1 * middle_stencil(m, e1_wide, mid)
    e0 = e0_wide[1:5, 1:7] + e1
    edge_y, edge_x = jnp.zeros((4, 1, 8, 128), F32), jnp.zeros((1, 8, 8, 128), F32)
    e0_rim = jnp.concatenate([edge_y, e0, edge_y], axis=1)
    e0_rim = jnp.concatenate([edge_x, e0_rim, edge_x], axis=0)
    precond_wide = e0 + e0_wide[1:5, 1:7] - dinv0 * stencil(m, e0_rim, wide)
    precond = precond_wide[1:3, 1:5]
    image_w = stencil(m, precond_wide, own_coef)
    precond8 = flat(precond)
    fields = jnp.concatenate([precond8, flat(own_p), flat(image_w), flat(image_p)], axis=0)
    with_locked = dot_split(fields, l_high[...], l_low[...], NT)
    f_pc, f_p, f_apc, f_ap = [fold_locked(m, with_locked[8 * i : 8 * i + 8]) for i in range(4)]
    cross = jnp.where(m.par0, jnp.where(m.half0, f_pc, f_apc), jnp.where(m.half0, f_p, f_ap))
    f_high, f_low = split(fields[:16])
    among = dot_split(fields, f_high, f_low, NT)
    row, col = iota((32, 16), 0), iota((32, 16), 1)
    among = jnp.where((row // 4) % 2 == (col // 4) % 2, among, 0.0)
    among = jnp.concatenate(
        [among[:16], jnp.zeros((16, 48), F32), among[16:], jnp.zeros((16, 48), F32)], axis=1
    )
    among = [among[:8], among[8:]]
    among = [u + subs(u, 4) for u in among]
    own = jnp.where(m.par0, among[0], among[1])
    own = own + lanes(own, -4)
    first = reduce_start(2, jnp.concatenate([cross, own], axis=0), by2)
    second_s = reduce_next(4, first_s, by3, bx3)
    late = reduce_end(2, first, by2, bx2) / cells
    cross, own = late[:8], late[8:]
    corr = jnp.where(in_use & m.half0 & m.par0, cross, 0.0)
    corr_ref[...] = corr[:ACTIVE, : corr_ref.shape[1]]
    twice = corr + subs(corr, 4)
    twice = twice + lanes(twice, 64)
    projected8 = precond8 - dot_split(spread_locked(m, twice), l_high[...], l_low[...], NN)
    trial_ref[...] = jnp.concatenate([x8, projected8, flat(own_p)], axis=0)
    second_s()
    inner = total([bx3[j] for j in range(ngx)]) / cells

    zero = jnp.zeros((8, 64), F32)
    low8 = iota((8, 64), 0) < 4
    spot = iota((8, 64), 1) == nl + iota((8, 64), 0)
    combine = jnp.concatenate([jnp.where(low8 & spot, 1.0, 0.0), -corr[:, :64], zero], axis=0)
    grams = []
    for i in range(2):
        cut = slice(64 * i, 64 * i + 64)
        part = cross[:, cut]
        direct = jnp.concatenate(
            [zero, jnp.where(low8, part, 0.0), jnp.where(low8, subs(part, 4), 0.0)], axis=0
        )
        gram = nt(nn(combine, inner[:, cut]) + direct, combine) + nt(combine, direct)
        some = own[:, 64 * i : 64 * i + 16]
        some = jnp.where((iota((8, 16), 1) // 4) % 2 == 0, some, 0.0)
        low16 = iota((8, 16), 0) < 4
        some = jnp.concatenate(
            [jnp.zeros((8, 16), F32), jnp.where(low16, some, 0.0), jnp.where(low16, subs(some, 4), 0.0)], axis=0
        )
        grams.append(gram + jnp.concatenate([jnp.zeros((24, 8), F32), some], axis=1))
    sums_ref[...] = jnp.concatenate(
        [grams[0], jnp.zeros((24, 8), F32), grams[1], jnp.zeros((24, 72), F32)], axis=1
    )

    everyone(lambda i, tx, ty: spread_out(i, tx, ty).wait_send())
    across(lambda d, j: rows_of(d, j).wait_send(), 1)
    for copy, to in pending:
        if to is None:
            copy.wait_send()
        else:
            pl.when(to)(copy.wait_send)


def finish(
    sums_hbm, trial_hbm, corr_hbm, new_modes_hbm, new_dirs_hbm, ritz_ref, corr_out,
    sums_ref, trial_ref, corr_ref, new_modes_ref, new_dirs_ref, sems,
):
    loads = [
        pltpu.make_async_copy(sums_hbm, sums_ref, sems.at[0]),
        pltpu.make_async_copy(trial_hbm, trial_ref, sems.at[1]),
        pltpu.make_async_copy(corr_hbm, corr_ref, sems.at[2]),
    ]
    for load in loads:
        load.start()
    m = Marks()
    row, col = iota((24, 128), 0), iota((24, 128), 1)
    for load in loads:
        load.wait()
    store_corr = pltpu.make_async_copy(corr_ref, corr_out, sems.at[3])
    store_corr.start()
    sums = sums_ref[...]
    real = row % 8 < 4
    table = jnp.where(real & (col < 64) & (col % 8 < 4), sums, 0.0)
    table = jnp.where(real & (col == row + 64), 1.0, table)
    pivots_at = [8 * g + f for g in range(3) for f in range(4)]

    def eliminate(work, order, rows):
        for k in order:
            pivot = work[k : k + 1, k : k + 1]
            scale = lax.rsqrt(pivot)
            line = work[k : k + 1, :] * scale
            factor = jnp.where(rows > k, work[:, k : k + 1] * scale, 0.0)
            work = jnp.where(rows == k, line, work - factor * line)
        return work

    work = eliminate(table, pivots_at, row)
    half = jnp.where(col < 24, lanes(work, -32), 0.0)
    linv = jnp.where(col < 24, lanes(work, -64), 0.0)
    reduced = 0.5 * (nt(half, linv) + nt(linv, half))
    reduced = jnp.concatenate([reduced, jnp.zeros((24, 104), F32)], axis=1)
    spectral = jnp.sum(jnp.where(row == col, reduced, 0.0), keepdims=True)
    raised = jnp.where((row == col) & real, spectral, 0.0) - reduced
    full = jnp.concatenate([raised, jnp.zeros((104, 128), F32)], axis=0)
    reduced_full = jnp.concatenate([reduced, jnp.zeros((104, 128), F32)], axis=0)
    basis = jnp.where(m.par0, raised[:8], 0.0)
    for step in range(RITZ - 1):
        basis = nn(basis, full)
    square = nt(basis, basis)
    small = jnp.concatenate([square, jnp.zeros((8, 120), F32)], axis=1) + lanes(basis, 32)
    small = eliminate(small, range(4), m.sub)
    basis = jnp.where((m.lane < 24) & m.par0, lanes(small, -32), 0.0)
    ritz = jnp.sum(basis * nn(basis, reduced_full), axis=1, keepdims=True)
    for k in range(ACTIVE):
        ritz_ref[k] = ritz[k, 0]
    linv_full = jnp.concatenate([linv, jnp.zeros((104, 128), F32)], axis=0)
    coef = nn(basis, linv_full)
    coef = coef + lanes(coef, 4)
    coef = coef + subs(coef, 4)
    coef = jnp.where(m.par0 == ((m.lane // 4) % 2 == 0), coef, 0.0)[:, :24]
    f_high, f_low = split(trial_ref[...])
    later = jnp.where(iota((8, 24), 1) >= 8, coef, 0.0)
    mixed = dot_split(jnp.concatenate([coef, later], axis=0), f_high, f_low, NN)
    modes8, dirs8 = mixed[:8], mixed[8:]
    for x in range(4):
        for y in range(4):
            cut = slice(128 * y, 128 * (y + 1))
            frm = slice(128 * ((x // 2) * 4 + y), 128 * ((x // 2) * 4 + y + 1))
            rows = slice(4 * (x % 2), 4 * (x % 2) + 4)
            new_modes_ref[:, x, cut] = modes8[rows, frm]
            new_dirs_ref[:, x, cut] = dirs8[rows, frm]
    stores = [
        pltpu.make_async_copy(new_modes_ref, new_modes_hbm, sems.at[4]),
        pltpu.make_async_copy(new_dirs_ref, new_dirs_hbm, sems.at[5]),
    ]
    for store in stores:
        store.start()
    for store in stores + [store_corr]:
        store.wait()


def on_device(ngx, ngy, modes, directions, locked, perm_class, perm_table, locked_count):
    vmem = pl.BlockSpec(memory_space=pltpu.VMEM)
    smem = pl.BlockSpec(memory_space=pltpu.SMEM)
    dma = pltpu.SemaphoreType.DMA
    wide = 2 * REACH + 1
    hbm = pl.BlockSpec(memory_space=pltpu.HBM)
    limit = 64 * 1024 * 1024 - 65536
    sums, trial, corr = pl.pallas_call(
        functools.partial(kernel, ngx, ngy),
        out_shape=(
            jax.ShapeDtypeStruct((24, 128), F32),
            jax.ShapeDtypeStruct((24, 1024), F32),
            jax.ShapeDtypeStruct((ACTIVE, locked.shape[0]), F32),
        ),
        in_specs=[hbm, hbm, hbm, hbm, smem, smem],
        out_specs=(vmem, vmem, vmem),
        scratch_shapes=[
            pltpu.VMEM((6, 8, 8, 128), F32),
            pltpu.VMEM((2, 4, 6, 8, 128), F32),
            pltpu.VMEM((6, 8, 8, 128), F32),
            pltpu.VMEM((6, 8, 8, 128), F32),
            pltpu.VMEM((wide, ngy, 8, 128), F32),
            pltpu.VMEM((wide, ngy, 4, 128), F32),
            pltpu.VMEM((2 * ngy + 2, 3, 4, 128), F32),
            pltpu.VMEM((64, 512), F32),
            pltpu.VMEM((64, 512), F32),
            pltpu.VMEM((128, 128), F32),
            pltpu.VMEM((128, 128), F32),
            pltpu.VMEM((2, 128, 128), F32),
            pltpu.VMEM((128, 1024), F32),
            pltpu.VMEM((128, 1024), F32),
            pltpu.VMEM((128, 1024), BF16),
            pltpu.VMEM((128, 1024), BF16),
            pltpu.VMEM(modes.shape, F32),
            pltpu.VMEM(directions.shape, F32),
            pltpu.VMEM(locked.shape, F32),
            pltpu.VMEM(perm_class.shape, jnp.int32),
            dma((4,)),
            pltpu.VMEM((ngx, ngy, 4, 128), F32),
            pltpu.VMEM((ngy, 16, 128), F32),
            pltpu.VMEM((ngx, 16, 128), F32),
            pltpu.VMEM((ngy, 64, 128), F32),
            pltpu.VMEM((ngx, 64, 128), F32),
            dma((5, 9)),
            dma((5, 9)),
            dma((8, max(ngx, ngy))),
            dma((8, max(ngx, ngy))),
            dma((2, wide)),
            dma((2, wide)),
            dma((ngx * ngy,)),
            dma((ngx * ngy,)),
            dma((wide, ngy)),
            dma((wide, ngy)),
        ],
        compiler_params=pltpu.CompilerParams(
            collective_id=0, has_side_effects=True, vmem_limit_bytes=limit
        ),
    )(modes, directions, locked, perm_class, perm_table, locked_count)
    new_modes, new_dirs, ritz, corr = pl.pallas_call(
        finish,
        out_shape=(
            jax.ShapeDtypeStruct(modes.shape, F32),
            jax.ShapeDtypeStruct(modes.shape, F32),
            jax.ShapeDtypeStruct((ACTIVE,), F32),
            jax.ShapeDtypeStruct(corr.shape, F32),
        ),
        in_specs=[hbm, hbm, hbm],
        out_specs=(hbm, hbm, smem, hbm),
        scratch_shapes=[
            pltpu.VMEM(sums.shape, F32),
            pltpu.VMEM(trial.shape, F32),
            pltpu.VMEM(corr.shape, F32),
            pltpu.VMEM(modes.shape, F32),
            pltpu.VMEM(modes.shape, F32),
            dma((6,)),
        ],
        compiler_params=pltpu.CompilerParams(vmem_limit_bytes=limit),
    )(sums, trial, corr)
    return new_modes, new_dirs, ritz, corr.T


def solution(mesh):
    placed = (
        P(None, "gx", "gy"),
        P(None, "gx", "gy"),
        P(None, "gx", "gy"),
        P("gx", "gy"),
        P(),
        P(),
    )
    return jax.shard_map(
        functools.partial(on_device, mesh.shape["gx"], mesh.shape["gy"]),
        mesh=mesh,
        in_specs=placed,
        out_specs=(P(None, "gx", "gy"), P(None, "gx", "gy"), P(), P()),
        check_vma=False,
    )
```

```python
import functools

import jax
import jax.numpy as jnp
from jax import lax
from jax.experimental import pallas as pl
from jax.experimental.pallas import tpu as pltpu
from jax.sharding import PartitionSpec as P

NZ = 64
ACTIVE = 4
SWEEPS = 3
RITZ = 3
OMEGA = 0.6
EPSILON = 1e-06
PRECISE = lax.Precision.HIGHEST
F32 = jnp.float32
REACH = SWEEPS


def iota(shape, dim):
    return lax.broadcasted_iota(jnp.int32, shape, dim)


def nt(a, b):
    return lax.dot_general(a, b, (((1,), (1,)), ((), ())), precision=PRECISE, preferred_element_type=F32)


def nn(a, b):
    return lax.dot_general(a, b, (((1,), (0,)), ((), ())), precision=PRECISE, preferred_element_type=F32)


def lanes(u, by):
    return pltpu.roll(u, by % 128, u.ndim - 1)


def subs(u, by):
    return pltpu.roll(u, by % 8, u.ndim - 2)


def face_value(a, b):
    both = (a > 0) & (b > 0)
    return jnp.where(both, 2.0 * a * b / jnp.where(both, a + b, 1.0), 2.0 * (a + b))


BF16 = jnp.bfloat16


def split(a):
    high = a.astype(BF16)
    return high, (a - high.astype(F32)).astype(BF16)


def dot_split(a, b_high, b_low, dims):
    rows = a.shape[0]
    high = a.astype(BF16).astype(F32)
    stack = jnp.concatenate([high, a - high], axis=0).astype(BF16)
    dims = (dims, ((), ()))
    one = lax.dot_general(stack, b_high, dims, preferred_element_type=F32)
    two = lax.dot_general(high.astype(BF16), b_low, dims, preferred_element_type=F32)
    return one[:rows] + (one[rows:] + two)


NT = ((1,), (1,))
NN = ((1,), (0,))


class Marks:
    def __init__(self):
        lane = iota((8, 128), 1)
        sub = iota((8, 128), 0)
        self.lane = lane
        self.sub = sub
        self.z = lane % NZ
        self.half0 = lane < 64
        self.par0 = sub < 4
        self.even = lane % 2 == 0
        self.quad = lane % 4 < 2


def neighbours(m, u):
    inner = u[1:-1, 1:-1]
    zl = jnp.where(m.z == 0, 0.0, lanes(inner, 1))
    zu = jnp.where(m.z == NZ - 1, 0.0, lanes(inner, -1))
    flip = lanes(u[1:-1], 64)
    yl = jnp.where(m.half0, flip[:, :-2], flip[:, 1:-1])
    yu = jnp.where(m.half0, flip[:, 1:-1], flip[:, 2:])
    turn = subs(u[:, 1:-1], 4)
    xl = jnp.where(m.par0, turn[:-2], turn[1:-1])
    xu = jnp.where(m.par0, turn[1:-1], turn[2:])
    return xl, xu, yl, yu, zl, zu


def total(parts):
    out = parts[0]
    for part in parts[1:]:
        out = out + part
    return out


def fine_coef(m, k):
    inner = k[1:-1, 1:-1]
    faces = [face_value(near, inner) for near in neighbours(m, k)]
    return [total(faces)] + faces


def stencil(m, u, coef):
    near = neighbours(m, u)
    return coef[0] * u[1:-1, 1:-1] - total([c * v for c, v in zip(coef[1:], near)])


def inverse(diag, inside):
    return jnp.where(inside, OMEGA / jnp.where(inside, diag, 1.0), 0.0)


def pair_x(u):
    return u + subs(u, 4)


def pair_y(u):
    return u + lanes(u, 64)


def pair_z(m, u):
    return u + jnp.where(m.even, lanes(u, -1), lanes(u, 1))


def pair_z2(m, u):
    return u + jnp.where(m.quad, lanes(u, -2), lanes(u, 2))


def middle_coef(m, c):
    xl = pair_z(m, pair_y(jnp.where(m.par0, c[1], subs(c[1], 4))))
    xu = pair_z(m, pair_y(jnp.where(m.par0, subs(c[2], 4), c[2])))
    yl = pair_z(m, pair_x(jnp.where(m.half0, c[3], lanes(c[3], 64))))
    yu = pair_z(m, pair_x(jnp.where(m.half0, lanes(c[4], 64), c[4])))
    zl = pair_y(pair_x(jnp.where(m.even, c[5], lanes(c[5], 1))))
    zu = pair_y(pair_x(jnp.where(m.even, lanes(c[6], -1), c[6])))
    faces = [xl, xu, yl, yu, zl, zu]
    return [total(faces)] + faces


def middle_stencil(m, u, coef):
    inner = u[1:-1, 1:-1]
    zl = jnp.where(m.z < 2, 0.0, lanes(inner, 2))
    zu = jnp.where(m.z >= NZ - 2, 0.0, lanes(inner, -2))
    near = [u[:-2, 1:-1], u[2:, 1:-1], u[1:-1, :-2], u[1:-1, 2:], zl, zu]
    return coef[0] * inner - total([c * v for c, v in zip(coef[1:], near)])


def coarse_pack(m, mid):
    _, xl, xu, yl, yu, zl, zu = mid
    out = jnp.zeros((8, 128), F32)
    for q in range(2):
        a, b = 2 * q, 2 * q + 1
        faces = [
            pair_z2(m, xl[0, a] + xl[0, b]),
            pair_z2(m, xu[1, a] + xu[1, b]),
            pair_z2(m, yl[0, a] + yl[1, a]),
            pair_z2(m, yu[0, b] + yu[1, b]),
        ]
        low = zl[0, a] + zl[0, b] + zl[1, a] + zl[1, b]
        high = zu[0, a] + zu[0, b] + zu[1, a] + zu[1, b]
        faces.append(jnp.where(m.quad, low, lanes(low, 2)))
        faces.append(jnp.where(m.quad, lanes(high, -2), high))
        for k in range(6):
            spot = (m.sub == 4 * q + k % 4) & (m.half0 if k < 4 else ~m.half0)
            out = jnp.where(spot, faces[k], out)
    return out


def flat(u):
    return jnp.concatenate([u[x, y] for x in range(2) for y in range(4)], axis=1)


def unflat(u):
    tiles = [u[:, 128 * i : 128 * (i + 1)] for i in range(8)]
    return jnp.stack([jnp.stack(tiles[:4]), jnp.stack(tiles[4:])])


def fold_locked(m, g):
    g = jnp.where(m.par0 == m.half0, g, 0.0)
    return pair_y(pair_x(g))


def spread_locked(m, c):
    return jnp.where(m.par0 == m.half0, c, 0.0)


def kernel(
    ngx,
    ngy,
    modes_hbm,
    dirs_hbm,
    locked_hbm,
    class_hbm,
    table_ref,
    count_ref,
    sums_ref,
    trial_ref,
    corr_ref,
    kh,
    xp,
    e0h,
    e1h,
    ccg,
    r2g,
    e2s,
    lxlow,
    lxhigh,
    lylow,
    lyhigh,
    lysend,
    al,
    lst,
    l_high,
    l_low,
    modes_ref,
    dirs_ref,
    locked_ref,
    class_ref,
    ins,
    by1,
    by2,
    bx2,
    by3,
    bx3,
    hs,
    hr,
    rs,
    rr,
    cs,
    cr,
    os,
    orr,
    gs,
    gr,
):
    loads = [
        pltpu.make_async_copy(src, dst, ins.at[i])
        for i, (src, dst) in enumerate(
            [(class_hbm, class_ref), (modes_hbm, modes_ref), (dirs_hbm, dirs_ref), (locked_hbm, locked_ref)]
        )
    ]
    for load in loads:
        load.start()
    m = Marks()
    gx, gy = lax.axis_index("gx"), lax.axis_index("gy")
    count = ngx * ngy
    cells = float(4 * 512 * count)
    pending = []

    for buf in (kh, xp, e0h, e1h, ccg, r2g, e2s, lxlow, lxhigh, lylow, lyhigh):
        buf[...] = jnp.zeros(buf.shape, F32)

    barrier = pltpu.get_barrier_semaphore()

    def greet(tx, ty):
        pl.semaphore_signal(barrier, inc=1, device_id=(tx, ty), device_id_type=pl.DeviceIdType.MESH)

    def everyone(visit):
        if count <= 64:
            for i in range(1, count):
                visit(i, lax.rem(gx + i // ngy, ngx), lax.rem(gy + i % ngy, ngy))
        else:

            def body(i, carry):
                visit(i, lax.rem(gx + i // ngy, ngx), lax.rem(gy + lax.rem(i, ngy), ngy))
                return carry

            lax.fori_loop(1, count, body, 0)

    everyone(lambda i, tx, ty: greet(tx, ty))

    def remote(src, dst, send, recv, tx, ty):
        return pltpu.make_async_remote_copy(
            src_ref=src, dst_ref=dst, send_sem=send, recv_sem=recv, device_id=(tx, ty),
            device_id_type=pl.DeviceIdType.MESH,
        )

    def inside(tx, ty):
        return (tx >= 0) & (tx < ngx) & (ty >= 0) & (ty < ngy)

    def halo(slot, view, w, corners):
        def span(d, n):
            if d > 0:
                return pl.ds(n, w), pl.ds(0, w)
            if d < 0:
                return pl.ds(w, w), pl.ds(w + n, w)
            return pl.ds(w, n), pl.ds(w, n)

        copies = []
        for dx in (-1, 0, 1):
            for dy in (-1, 0, 1):
                if (dx, dy) == (0, 0) or (dx and dy and not corners):
                    continue
                (sx, tx), (sy, ty) = span(dx, 2), span(dy, 4)
                n = (dx + 1) * 3 + dy + 1
                copy = remote(view(sx, sy), view(tx, ty), hs.at[slot, n], hr.at[slot, n], gx + dx, gy + dy)
                to, frm = inside(gx + dx, gy + dy), inside(gx - dx, gy - dy)
                pl.when(to)(copy.start)
                copies.append((copy, frm))
                pending.append((copy, to))

        def arrive():
            for copy, frm in copies:
                pl.when(frm)(copy.wait_recv)

        return arrive

    def share(slot, buf, mine, n, axis, view):
        copies = []
        for i in range(1, n):
            to, frm = lax.rem(mine + i, n), lax.rem(mine + n - i, n)
            where = (gx, to) if axis == "gy" else (to, gy)
            back = (gx, frm) if axis == "gy" else (frm, gy)
            copy = remote(view(buf, mine), view(buf, mine), rs.at[slot, i], rr.at[slot, i], *where)
            copy.start()
            pending.append((copy, None))
            copies.append(remote(view(buf, frm), view(buf, frm), rs.at[slot, i], rr.at[slot, i], *back))

        def arrive():
            for copy in copies:
                copy.wait_recv()

        return arrive

    def spread_out(i, tx, ty):
        return remote(by1.at[gx, gy], by1.at[gx, gy], os.at[i], orr.at[i], tx, ty)

    def spread_in(i, tx, ty):
        fx = lax.rem(gx + ngx - i // ngy, ngx)
        fy = lax.rem(gy + ngy - (i % ngy if isinstance(i, int) else lax.rem(i, ngy)), ngy)
        return remote(by1.at[fx, fy], by1.at[fx, fy], os.at[i], orr.at[i], fx, fy)

    def rows_of(d, j):
        ty = lax.rem(gy + j, ngy)
        return remote(
            r2g.at[REACH, gy], r2g.at[REACH - d, gy], gs.at[d + REACH, j], gr.at[d + REACH, j], gx + d, ty
        )

    def rows_in(d, j):
        fy = lax.rem(gy + ngy - j, ngy)
        return remote(
            r2g.at[REACH, fy], r2g.at[REACH - d, fy], gs.at[d + REACH, j], gr.at[d + REACH, j], gx - d, fy
        )

    def across(visit, sign):
        for d in range(-REACH, REACH + 1):
            def row(d=d):
                for j in range(ngy):
                    if (d, j) != (0, 0):
                        visit(d, j)

            if d == 0:
                row()
            else:
                pl.when((gx + sign * d >= 0) & (gx + sign * d < ngx))(row)

    def reduce_start(slot, val, bufy):
        bufy[gy] = val
        return share(slot, bufy, gy, ngy, "gy", lambda b, i: b.at[i])

    def reduce_next(slot, first, bufy, bufx):
        first()
        bufx[gx] = total([bufy[j] for j in range(ngy)])
        return share(slot + 1, bufx, gx, ngx, "gx", lambda b, i: b.at[i])

    def reduce_end(slot, first, bufy, bufx):
        reduce_next(slot, first, bufy, bufx)()
        return total([bufx[j] for j in range(ngx)])

    def gather_start(slot, buf, val):
        buf[REACH, gy] = val
        return share(slot, buf, gy, ngy, "gy", lambda b, i: b.at[REACH, i])

    def gather_next(slot, first, buf):
        first()
        copies = []
        for d in range(-REACH, REACH + 1):
            if d == 0:
                continue
            copy = remote(
                buf.at[REACH], buf.at[REACH - d], cs.at[slot, d + REACH], cr.at[slot, d + REACH], gx + d, gy
            )
            to, frm = inside(gx + d, gy), inside(gx - d, gy)
            pl.when(to)(copy.start)
            copies.append((copy, frm))
            pending.append((copy, to))

        def arrive():
            for copy, frm in copies:
                pl.when(frm)(copy.wait_recv)

        return arrive

    for load in loads[:3]:
        load.wait()
    classes = class_ref[...]
    conduct = jnp.zeros(classes.shape, F32)
    for c in range(table_ref.shape[0]):
        conduct = jnp.where(classes == c, table_ref[c], conduct)
    for x in range(4):
        for y in range(4):
            cut = slice(128 * y, 128 * (y + 1))
            rows = pl.ds(4 * (x % 2), 4)
            kh[2 + x // 2, 2 + y, rows, :] = jnp.broadcast_to(conduct[x : x + 1, cut], (4, 128))
            xp[0, 1 + x // 2, 1 + y, rows, :] = modes_ref[:, x, cut]
            xp[1, 1 + x // 2, 1 + y, rows, :] = dirs_ref[:, x, cut]
    pl.semaphore_wait(barrier, count - 1)
    arrive_k = halo(0, lambda a, b: kh.at[a, b], 2, True)
    arrive_xp = halo(1, lambda a, b: xp.at[:, a, b], 1, False)

    loads[3].wait()
    nl = locked_ref.shape[0]
    for x in range(4):
        for y in range(4):
            cut = slice(128 * y, 128 * (y + 1))
            to = pl.ds(128 * ((x // 2) * 4 + y), 128)
            lst[pl.ds(64 * (x % 2), nl), to] = locked_ref[:, x, cut]
            lst[pl.ds(64 * (x % 2) + nl, 4), to] = modes_ref[:, x, cut]

    def tile(x, y, par):
        return lst[64 * par : 64 * par + 64, 128 * (4 * x + y) : 128 * (4 * x + y) + 128]

    def column(x, y):
        return lst[:, 128 * (4 * x + y) : 128 * (4 * x + y) + 128]

    wide_lane = iota((128, 128), 1) < 64
    lysend[0] = jnp.where(wide_lane, lanes(column(0, 3), 64), column(1, 3))
    lysend[1] = jnp.where(wide_lane, column(0, 0), lanes(column(1, 0), 64))
    locked_copies = []
    for n, (src, dst, dx, dy) in enumerate(
        [
            (lst.at[pl.ds(64, 64), pl.ds(512, 512)], lxlow, 1, 0),
            (lst.at[pl.ds(0, 64), pl.ds(0, 512)], lxhigh, -1, 0),
            (lysend.at[0], lylow, 0, 1),
            (lysend.at[1], lyhigh, 0, -1),
        ]
    ):
        copy = remote(src, dst, hs.at[4, n], hr.at[4, n], gx + dx, gy + dy)
        to, frm = inside(gx + dx, gy + dy), inside(gx - dx, gy - dy)
        pl.when(to)(copy.start)
        pending.append((copy, to))
        locked_copies.append((copy, frm))

    own_x = xp[0, 1:3, 1:5]
    own_p = xp[1, 1:3, 1:5]
    x8 = flat(own_x)
    high, low = split(lst[...])
    l_high[...] = high
    l_low[...] = low
    mode_dots = fold_locked(m, dot_split(x8, l_high[...], l_low[...], NT))

    arrive_k()
    arrive_xp()
    own_coef = fine_coef(m, kh[1:5, 1:7])
    image_x = stencil(m, xp[0], own_coef)
    image_x8 = flat(image_x)
    image_dots = fold_locked(m, dot_split(image_x8, l_high[...], l_low[...], NT))
    by1[gx, gy] = jnp.where(m.half0, image_dots, mode_dots)[:4]
    everyone(lambda i, tx, ty: spread_out(i, tx, ty).start())

    wide = fine_coef(m, kh[...])
    in_grid = kh[1:5, 1:7] > 0
    dinv0 = inverse(wide[0], in_grid)
    mid = middle_coef(m, wide)
    dinv1 = inverse(mid[0], in_grid)
    own_mid = [c[1:3, 1:5] for c in mid]
    first_c = gather_start(6, ccg, coarse_pack(m, own_mid))
    image_p = stencil(m, xp[1], own_coef)
    everyone(lambda i, tx, ty: spread_in(i, tx, ty).wait_recv())
    sums = jnp.sum(by1[...].reshape(count, 4, 128), axis=0)
    sums = jnp.concatenate([sums, sums], axis=0)

    f_of = m.sub % 4
    top = jnp.sum(jnp.where(m.lane == nl + f_of, sums, 0.0), axis=1, keepdims=True)
    norm = jnp.sum(jnp.where(m.lane == 64 + nl + f_of, sums, 0.0), axis=1, keepdims=True)
    rayleigh = top / cells / (norm / cells + EPSILON)
    swapped = lanes(sums, 64)
    image_sum = jnp.where(m.half0, sums, swapped)
    mode_sum = jnp.where(m.half0, swapped, sums)
    j_of = m.lane % 64
    in_use = (j_of < count_ref[0]) & (j_of < nl)
    coupling = jnp.where(in_use, (image_sum - mode_sum * rayleigh) / cells, 0.0)
    coupling = jnp.where(j_of == nl + f_of, rayleigh, coupling)
    residual = image_x - unflat(
        dot_split(spread_locked(m, coupling), l_high[...], l_low[...], NN)
    )

    e0h[2:4, 2:6] = residual * dinv0[1:3, 1:5]
    arrive_e0 = halo(2, lambda a, b: e0h.at[a, b], 2, True)
    arrive_c = gather_next(0, first_c, ccg)
    for copy, frm in locked_copies:
        pl.when(frm)(copy.wait_recv)
    low64 = iota((64, 128), 1) < 64
    z_row = iota((1, 128), 1) % NZ
    for x in range(2):
        for par in range(2):
            rows = slice(64 * par, 64 * par + 64)
            flips = [lanes(tile(x, y, par), 64) for y in range(4)]
            before = lylow[rows] if x == 0 else lanes(lylow[rows], 64)
            after = lyhigh[rows] if x == 1 else lanes(lyhigh[rows], 64)
            flips = [before] + flips + [after]
            for y in range(4):
                u = tile(x, y, par)
                cut = slice(128 * y, 128 * y + 128)
                if par:
                    xl = tile(x, y, 0)
                    xu = tile(1, y, 0) if x == 0 else lxhigh[:, cut]
                else:
                    xl = tile(0, y, 1) if x == 1 else lxlow[:, cut]
                    xu = tile(x, y, 1)
                yl = jnp.where(low64, flips[y], flips[y + 1])
                yu = jnp.where(low64, flips[y + 1], flips[y + 2])
                c = [k[x, y, 4 * par : 4 * par + 1] for k in own_coef]
                near = c[1] * xl + c[2] * xu + c[3] * yl + c[4] * yu
                near = near + jnp.where(z_row == 0, 0.0, c[5]) * lanes(u, 1)
                near = near + jnp.where(z_row == NZ - 1, 0.0, c[6]) * lanes(u, -1)
                al[rows, 128 * (4 * x + y) : 128 * (4 * x + y) + 128] = c[0] * u - near

    arrive_e0()
    e0_wide = e0h[...]
    r1 = e0_wide[1:5, 1:7] * (wide[0] * (1.0 / OMEGA)) - stencil(m, e0_wide, wide)
    r1 = pair_z(m, pair_y(pair_x(r1)))
    e1_near = r1 * dinv1
    e1h[2:4, 2:6] = e1_near[1:3, 1:5]
    arrive_e1 = halo(3, lambda a, b: e1h.at[a, b], 2, True)
    r2 = r1[1:3, 1:5] - middle_stencil(m, e1_near, own_mid)
    r2 = r2[0] + r2[1]
    r2 = jnp.where(m.half0, r2[0] + r2[1], r2[2] + r2[3])
    r2g[REACH, gy] = pair_z2(m, r2)[:4]
    across(lambda d, j: rows_of(d, j).start(), 1)
    arrive_c()
    lines = 2 * ngy
    shift = 4.0 / float(lines * lines)
    faces = []
    for y in range(lines):
        tile = ccg[:, y // 2]
        other = lanes(tile, 64)
        low, high = jnp.where(m.half0, tile, other), jnp.where(m.half0, other, tile)
        row = 4 * (y % 2)
        one = []
        for k in range(6):
            src = low if k < 4 else high
            one.append(jnp.broadcast_to(src[:, row + k % 4 : row + k % 4 + 1], (2 * REACH + 1, 4, 128)))
        faces.append(one)
    z4 = m.z[:4]
    pivots, uppers, diags, dinv2 = [], [], [], []
    for y in range(lines):
        xl, xu, yl, yu, zl, zu = faces[y]
        diag = xl + xu + yl + yu + zl + zu
        known = diag > 0
        main = yl + yu + shift * (xl + xu + zl + zu)
        if y:
            main = main - yl * uppers[y - 1]
        piv = 1.0 / jnp.where(known, main, 1.0)
        pivots.append(piv)
        uppers.append(yu * piv)
        diags.append(diag)
        dinv2.append(inverse(diag, known))
        faces[y][4] = jnp.where(z4 < 4, 0.0, zl)
        faces[y][5] = jnp.where(z4 >= NZ - 4, 0.0, zu)

    square = []
    for left in (lst[...], al[...]):
        whole = dot_split(left, l_high[...], l_low[...], NT)
        square.append(whole[:64, :64] + whole[64:, 64:])
    first_s = reduce_start(4, jnp.concatenate(square, axis=1), by3)
    across(lambda d, j: rows_in(d, j).wait_recv(), -1)

    source = []
    for y in range(lines):
        tile_y = r2g[:, y // 2]
        other = lanes(tile_y, 64)
        source.append(jnp.where(m.half0[:4], *((tile_y, other) if y % 2 == 0 else (other, tile_y))))
    held = []
    for y in range(lines):
        right = source[y] if y == 0 else source[y] + faces[y][2] * held[y - 1]
        held.append(right * pivots[y])
    for y in range(lines - 2, -1, -1):
        held[y] = held[y] + uppers[y] * held[y + 1]
    for sweep in range(1, SWEEPS):
        nxt = []
        for y in range(lines):
            cut = slice(sweep, 2 * REACH + 1 - sweep)
            c = [f[cut] for f in faces[y]]
            u = held[y]
            mid_u = u[1:-1]
            beside = c[0] * u[:-2] + c[1] * u[2:]
            if y:
                beside = beside + c[2] * held[y - 1][1:-1]
            if y < lines - 1:
                beside = beside + c[3] * held[y + 1][1:-1]
            beside = beside + c[4] * lanes(mid_u, 4) + c[5] * lanes(mid_u, -4)
            off = source[y][cut] - (diags[y][cut] * mid_u - beside)
            nxt.append(mid_u + dinv2[y][cut] * off)
        held = nxt
    for y in range(lines):
        e2s[1 + y] = held[y]
    near = e2s[pl.ds(2 * gy, 4)]
    near = jnp.concatenate([near, near], axis=2)

    second_s = reduce_next(4, first_s, by3, bx3)
    arrive_e1()
    e1_wide = e1h[...]
    e1_wide = jnp.stack(
        [jnp.stack([e1_wide[a, b] + near[b // 2, a // 2] for b in range(8)]) for a in range(6)]
    )
    e1 = e1_wide[1:5, 1:7] + e1h[1:5, 1:7] - dinv1 * middle_stencil(m, e1_wide, mid)
    e0 = e0_wide[1:5, 1:7] + e1
    edge_y, edge_x = jnp.zeros((4, 1, 8, 128), F32), jnp.zeros((1, 8, 8, 128), F32)
    e0_rim = jnp.concatenate([edge_y, e0, edge_y], axis=1)
    e0_rim = jnp.concatenate([edge_x, e0_rim, edge_x], axis=0)
    precond_wide = e0 + e0_wide[1:5, 1:7] - dinv0 * stencil(m, e0_rim, wide)
    precond = precond_wide[1:3, 1:5]
    image_w = stencil(m, precond_wide, own_coef)
    precond8 = flat(precond)
    fields = jnp.concatenate([precond8, flat(own_p), flat(image_w), flat(image_p)], axis=0)
    with_locked = dot_split(fields, l_high[...], l_low[...], NT)
    f_pc, f_p, f_apc, f_ap = [fold_locked(m, with_locked[8 * i : 8 * i + 8]) for i in range(4)]
    cross = jnp.where(m.par0, jnp.where(m.half0, f_pc, f_apc), jnp.where(m.half0, f_p, f_ap))
    f_high, f_low = split(fields[:16])
    among = dot_split(fields, f_high, f_low, NT)
    row, col = iota((32, 16), 0), iota((32, 16), 1)
    among = jnp.where((row // 4) % 2 == (col // 4) % 2, among, 0.0)
    among = jnp.concatenate(
        [among[:16], jnp.zeros((16, 48), F32), among[16:], jnp.zeros((16, 48), F32)], axis=1
    )
    among = [among[:8], among[8:]]
    among = [u + subs(u, 4) for u in among]
    own = jnp.where(m.par0, among[0], among[1])
    own = own + lanes(own, -4)
    first = reduce_start(2, jnp.concatenate([cross, own], axis=0), by2)
    late = reduce_end(2, first, by2, bx2) / cells
    cross, own = late[:8], late[8:]
    corr = jnp.where(in_use & m.half0 & m.par0, cross, 0.0)
    corr_ref[...] = corr[:ACTIVE, : corr_ref.shape[1]]
    twice = corr + subs(corr, 4)
    twice = twice + lanes(twice, 64)
    projected8 = precond8 - dot_split(spread_locked(m, twice), l_high[...], l_low[...], NN)
    trial_ref[...] = jnp.concatenate([x8, projected8, flat(own_p)], axis=0)
    second_s()
    inner = total([bx3[j] for j in range(ngx)]) / cells

    zero = jnp.zeros((8, 64), F32)
    low8 = iota((8, 64), 0) < 4
    spot = iota((8, 64), 1) == nl + iota((8, 64), 0)
    combine = jnp.concatenate([jnp.where(low8 & spot, 1.0, 0.0), -corr[:, :64], zero], axis=0)
    grams = []
    for i in range(2):
        cut = slice(64 * i, 64 * i + 64)
        part = cross[:, cut]
        direct = jnp.concatenate(
            [zero, jnp.where(low8, part, 0.0), jnp.where(low8, subs(part, 4), 0.0)], axis=0
        )
        gram = nt(nn(combine, inner[:, cut]) + direct, combine) + nt(combine, direct)
        some = own[:, 64 * i : 64 * i + 16]
        some = jnp.where((iota((8, 16), 1) // 4) % 2 == 0, some, 0.0)
        low16 = iota((8, 16), 0) < 4
        some = jnp.concatenate(
            [jnp.zeros((8, 16), F32), jnp.where(low16, some, 0.0), jnp.where(low16, subs(some, 4), 0.0)], axis=0
        )
        grams.append(gram + jnp.concatenate([jnp.zeros((24, 8), F32), some], axis=1))
    sums_ref[...] = jnp.concatenate(
        [grams[0], jnp.zeros((24, 8), F32), grams[1], jnp.zeros((24, 72), F32)], axis=1
    )

    everyone(lambda i, tx, ty: spread_out(i, tx, ty).wait_send())
    across(lambda d, j: rows_of(d, j).wait_send(), 1)
    for copy, to in pending:
        if to is None:
            copy.wait_send()
        else:
            pl.when(to)(copy.wait_send)


def finish(
    sums_hbm, trial_hbm, corr_hbm, new_modes_hbm, new_dirs_hbm, ritz_ref, corr_out,
    sums_ref, trial_ref, corr_ref, new_modes_ref, new_dirs_ref, sems,
):
    loads = [
        pltpu.make_async_copy(sums_hbm, sums_ref, sems.at[0]),
        pltpu.make_async_copy(trial_hbm, trial_ref, sems.at[1]),
        pltpu.make_async_copy(corr_hbm, corr_ref, sems.at[2]),
    ]
    for load in loads:
        load.start()
    m = Marks()
    row, col = iota((24, 128), 0), iota((24, 128), 1)
    for load in loads:
        load.wait()
    store_corr = pltpu.make_async_copy(corr_ref, corr_out, sems.at[3])
    store_corr.start()
    sums = sums_ref[...]
    real = row % 8 < 4
    table = jnp.where(real & (col < 64) & (col % 8 < 4), sums, 0.0)
    table = jnp.where(real & (col == row + 64), 1.0, table)
    pivots_at = [8 * g + f for g in range(3) for f in range(4)]

    def eliminate(work, order, rows):
        for k in order:
            pivot = work[k : k + 1, k : k + 1]
            scale = lax.rsqrt(pivot)
            line = work[k : k + 1, :] * scale
            factor = jnp.where(rows > k, work[:, k : k + 1] * scale, 0.0)
            work = jnp.where(rows == k, line, work - factor * line)
        return work

    work = eliminate(table, pivots_at, row)
    half = jnp.where(col < 24, lanes(work, -32), 0.0)
    linv = jnp.where(col < 24, lanes(work, -64), 0.0)
    reduced = 0.5 * (nt(half, linv) + nt(linv, half))
    reduced = jnp.concatenate([reduced, jnp.zeros((24, 104), F32)], axis=1)
    spectral = jnp.sum(jnp.where(row == col, reduced, 0.0), keepdims=True)
    raised = jnp.where((row == col) & real, spectral, 0.0) - reduced
    full = jnp.concatenate([raised, jnp.zeros((104, 128), F32)], axis=0)
    reduced_full = jnp.concatenate([reduced, jnp.zeros((104, 128), F32)], axis=0)
    basis = jnp.where(m.par0, raised[:8], 0.0)
    for step in range(RITZ - 1):
        basis = nn(basis, full)
    square = nt(basis, basis)
    small = jnp.concatenate([square, jnp.zeros((8, 120), F32)], axis=1) + lanes(basis, 32)
    small = eliminate(small, range(4), m.sub)
    basis = jnp.where((m.lane < 24) & m.par0, lanes(small, -32), 0.0)
    ritz = jnp.sum(basis * nn(basis, reduced_full), axis=1, keepdims=True)
    for k in range(ACTIVE):
        ritz_ref[k] = ritz[k, 0]
    linv_full = jnp.concatenate([linv, jnp.zeros((104, 128), F32)], axis=0)
    coef = nn(basis, linv_full)
    coef = coef + lanes(coef, 4)
    coef = coef + subs(coef, 4)
    coef = jnp.where(m.par0 == ((m.lane // 4) % 2 == 0), coef, 0.0)[:, :24]
    f_high, f_low = split(trial_ref[...])
    later = jnp.where(iota((8, 24), 1) >= 8, coef, 0.0)
    mixed = dot_split(jnp.concatenate([coef, later], axis=0), f_high, f_low, NN)
    modes8, dirs8 = mixed[:8], mixed[8:]
    for x in range(4):
        for y in range(4):
            cut = slice(128 * y, 128 * (y + 1))
            frm = slice(128 * ((x // 2) * 4 + y), 128 * ((x // 2) * 4 + y + 1))
            rows = slice(4 * (x % 2), 4 * (x % 2) + 4)
            new_modes_ref[:, x, cut] = modes8[rows, frm]
            new_dirs_ref[:, x, cut] = dirs8[rows, frm]
    stores = [
        pltpu.make_async_copy(new_modes_ref, new_modes_hbm, sems.at[4]),
        pltpu.make_async_copy(new_dirs_ref, new_dirs_hbm, sems.at[5]),
    ]
    for store in stores:
        store.start()
    for store in stores + [store_corr]:
        store.wait()


def on_device(ngx, ngy, modes, directions, locked, perm_class, perm_table, locked_count):
    vmem = pl.BlockSpec(memory_space=pltpu.VMEM)
    smem = pl.BlockSpec(memory_space=pltpu.SMEM)
    dma = pltpu.SemaphoreType.DMA
    wide = 2 * REACH + 1
    hbm = pl.BlockSpec(memory_space=pltpu.HBM)
    limit = 64 * 1024 * 1024 - 65536
    sums, trial, corr = pl.pallas_call(
        functools.partial(kernel, ngx, ngy),
        out_shape=(
            jax.ShapeDtypeStruct((24, 128), F32),
            jax.ShapeDtypeStruct((24, 1024), F32),
            jax.ShapeDtypeStruct((ACTIVE, locked.shape[0]), F32),
        ),
        in_specs=[hbm, hbm, hbm, hbm, smem, smem],
        out_specs=(vmem, vmem, vmem),
        scratch_shapes=[
            pltpu.VMEM((6, 8, 8, 128), F32),
            pltpu.VMEM((2, 4, 6, 8, 128), F32),
            pltpu.VMEM((6, 8, 8, 128), F32),
            pltpu.VMEM((6, 8, 8, 128), F32),
            pltpu.VMEM((wide, ngy, 8, 128), F32),
            pltpu.VMEM((wide, ngy, 4, 128), F32),
            pltpu.VMEM((2 * ngy + 2, 3, 4, 128), F32),
            pltpu.VMEM((64, 512), F32),
            pltpu.VMEM((64, 512), F32),
            pltpu.VMEM((128, 128), F32),
            pltpu.VMEM((128, 128), F32),
            pltpu.VMEM((2, 128, 128), F32),
            pltpu.VMEM((128, 1024), F32),
            pltpu.VMEM((128, 1024), F32),
            pltpu.VMEM((128, 1024), BF16),
            pltpu.VMEM((128, 1024), BF16),
            pltpu.VMEM(modes.shape, F32),
            pltpu.VMEM(directions.shape, F32),
            pltpu.VMEM(locked.shape, F32),
            pltpu.VMEM(perm_class.shape, jnp.int32),
            dma((4,)),
            pltpu.VMEM((ngx, ngy, 4, 128), F32),
            pltpu.VMEM((ngy, 16, 128), F32),
            pltpu.VMEM((ngx, 16, 128), F32),
            pltpu.VMEM((ngy, 64, 128), F32),
            pltpu.VMEM((ngx, 64, 128), F32),
            dma((5, 9)),
            dma((5, 9)),
            dma((8, max(ngx, ngy))),
            dma((8, max(ngx, ngy))),
            dma((2, wide)),
            dma((2, wide)),
            dma((ngx * ngy,)),
            dma((ngx * ngy,)),
            dma((wide, ngy)),
            dma((wide, ngy)),
        ],
        compiler_params=pltpu.CompilerParams(
            collective_id=0, has_side_effects=True, vmem_limit_bytes=limit
        ),
    )(modes, directions, locked, perm_class, perm_table, locked_count)
    new_modes, new_dirs, ritz, corr = pl.pallas_call(
        finish,
        out_shape=(
            jax.ShapeDtypeStruct(modes.shape, F32),
            jax.ShapeDtypeStruct(modes.shape, F32),
            jax.ShapeDtypeStruct((ACTIVE,), F32),
            jax.ShapeDtypeStruct(corr.shape, F32),
        ),
        in_specs=[hbm, hbm, hbm],
        out_specs=(hbm, hbm, smem, hbm),
        scratch_shapes=[
            pltpu.VMEM(sums.shape, F32),
            pltpu.VMEM(trial.shape, F32),
            pltpu.VMEM(corr.shape, F32),
            pltpu.VMEM(modes.shape, F32),
            pltpu.VMEM(modes.shape, F32),
            dma((6,)),
        ],
        compiler_params=pltpu.CompilerParams(vmem_limit_bytes=limit),
    )(sums, trial, corr)
    return new_modes, new_dirs, ritz, corr.T


def solution(mesh):
    placed = (
        P(None, "gx", "gy"),
        P(None, "gx", "gy"),
        P(None, "gx", "gy"),
        P("gx", "gy"),
        P(),
        P(),
    )
    return jax.shard_map(
        functools.partial(on_device, mesh.shape["gx"], mesh.shape["gy"]),
        mesh=mesh,
        in_specs=placed,
        out_specs=(P(None, "gx", "gy"), P(None, "gx", "gy"), P(), P()),
        check_vma=False,
    )
```
